32 devices in a mesh: req: 16 (over z, y, x), tp: 2 (over core).
Axes of the slice: x: 2, y: 2, z: 4, core: 2. Of those that a mesh axis runs over, the one named last changes fastest.
Arguments:
- vit_context: bfloat16 [8192, 4096], P('req', 'tp'), may hold values from -6 to 6
- vision_residual: bfloat16 [8192, 4096], P('req', 'tp'), may hold values from -75 to 75
- out_weight: bfloat16 [4096, 4096], P('tp', 'req'), may hold values from -0.09375 to 0.09375
- layer_scale: float32 [4096], P('tp'), may hold values from 0.2 to 2
- prompt: bfloat16 [16, 256, 4096], P('req', None, 'tp'), may hold values from -75 to 75
- prompt_len: int32 [16], P('req'), may hold values from 128 to 256
- image_at: int32 [16], P('req'), may hold values from 0 to 128
- grid_sizes: int32 [32, 2], replicated, may hold values from 7 to 8, as said below
- image_owner: int32 [32], replicated, may hold values from 0 to 15, as said below
- norm_gain: float32 [4096], replicated, may hold values from 0.5 to 1.5
- qkv_weight: bfloat16 [4096, 6144], P('req', 'tp'), may hold values from -0.09375 to 0.09375
Outputs:
- qkv: bfloat16 [6144, 6144], P('req', 'tp')
The draws below stay inside these ranges and needn't reach their ends.
Inputs may be any that keep to these rules, and one draw needn't show every extreme that they name: `image_owner`: each request owns exactly 2 images. `grid_sizes`: each side is 7 or 8; in every draw the images of some request are all 8 by 8, so that request has exactly 128 merged rows.
All inputs are finite; a program needn't handle non-finite values.
Results may differ from the reference program's by a relative error of at most 0.008.
Values may be sent and summed in bfloat16 or wider, within the bound.
A program may use at most 64 MiB of HBM per device.

```python
import math
import jax
import jax.numpy as jnp
from jax import lax

D = 4096
HEAD = 128
GRID_MAX = 8
IMG_REQ = 2
PROMPT_MAX = 256
GROUP = 4
QKV = 6144
IMG_MAX = 128
MRG_DEV = 128
P_DEV = 512
SEQ = 384
REQS = 16
IMAGES = 32
PATCHES = 8192
N_TP = 2


def image_plan(key):
    order = jax.random.permutation(jax.random.fold_in(key, 11), IMAGES)
    image_owner = (order // IMG_REQ).astype(jnp.int32)
    chosen = jax.random.randint(jax.random.fold_in(key, 12), (), 0, REQS)
    sides = jax.random.randint(jax.random.fold_in(key, 13), (IMAGES, 2), GRID_MAX - 1, GRID_MAX + 1)
    sides = jnp.where((image_owner == chosen)[:, None], GRID_MAX, sides)
    return (image_owner, sides.astype(jnp.int32))


def draw_image_owner(key, part):
    return image_plan(key)[0]


def draw_grid_sizes(key, part):
    return image_plan(key)[1]


def scaled_rows(key, array_shape):
    key_list = jax.random.split(key, 3)
    raw_values = jax.random.normal(key_list[0], array_shape, jnp.float32)
    raw_values = jnp.clip(raw_values, -5.0, 5.0)
    row_draw = jax.random.uniform(key_list[1], array_shape[:-1] + (1,), jnp.float32)
    row_scale = jnp.exp(math.log(10.0) * (row_draw - 0.5))
    column_draw = jax.random.uniform(key_list[2], (array_shape[-1],), jnp.float32)
    column_scale = jnp.exp(math.log(10.0) * (column_draw - 0.5))
    return raw_values * row_scale * column_scale


def draw_prompt(key, part):
    return scaled_rows(key, (REQS, PROMPT_MAX, D)).astype(jnp.bfloat16)


def draw_vision_residual(key, part):
    return scaled_rows(key, (PATCHES, D)).astype(jnp.bfloat16)


def set_ends(array, rng, smallest, largest):
    shape = array.shape
    index_at = [jax.random.randint(jax.random.fold_in(rng, axis), (), 0, shape[axis]) for axis in range(len(shape))]
    array = array.at[tuple(index_at)].set(smallest)
    longest = shape.index(max(shape))
    index_at[longest] = (index_at[longest] + 1) % shape[longest]
    return array.at[tuple(index_at)].set(largest)


def block_levels(rng, shape, cuts, least, largest):
    def one(position, blocks):
        heights = jax.random.uniform(jax.random.fold_in(jax.random.fold_in(rng, 6), position), (blocks,), jnp.float32, least / len(cuts), largest / len(cuts))
        return jnp.repeat(jnp.exp(heights), shape[position] // blocks).reshape((-1,) + (1,) * (len(shape) - position - 1))

    factor_of = one(*cuts[0])
    for cut in cuts[1:]:
        factor_of = factor_of * one(*cut)
    return factor_of


def noise(rng, dims, width, bound, cuts=(), kind=jnp.bfloat16):
    drawn = width * jax.random.normal(rng, dims, jnp.float32)
    if cuts:
        drawn = drawn * block_levels(rng, dims, cuts, -0.22, 0.18)
    return jnp.clip(drawn, -bound, bound).astype(kind)


def setup_inputs(seed: int = 0) -> dict:
    seeds = jax.random.split(jax.random.key(seed), 12)
    return {
        "vit_context": noise(seeds[0], (PATCHES, D), 1.0, 6.0, ((0, 16), (1, 2))),
        "vision_residual": draw_vision_residual(jax.random.fold_in(seeds[11], 71), 0),
        "out_weight": noise(seeds[2], (D, D), D ** -0.5, 0.09375, ((0, 2), (1, 16))),
        "layer_scale": jnp.clip(jnp.exp(math.log(2.0) - 2.3025851 * jax.random.uniform(seeds[3], (D,), jnp.float32) ** block_levels(seeds[3], (D,), ((0, 2),), -0.2, 0.2)), 0.2, 2.0),
        "prompt": draw_prompt(jax.random.fold_in(seeds[11], 71), 0),
        "prompt_len": set_ends(jax.random.randint(seeds[5], (REQS,), PROMPT_MAX // 2, PROMPT_MAX + 1), jax.random.fold_in(seeds[5], 1), PROMPT_MAX // 2, PROMPT_MAX).astype(jnp.int32),
        "image_at": set_ends(jax.random.randint(seeds[6], (REQS,), 0, PROMPT_MAX // 2 + 1), jax.random.fold_in(seeds[6], 1), 0, (PROMPT_MAX // 2 + 1) - 1).astype(jnp.int32),
        "grid_sizes": draw_grid_sizes(jax.random.fold_in(seeds[11], 71), 0),
        "image_owner": draw_image_owner(jax.random.fold_in(seeds[11], 71), 0),
        "norm_gain": jnp.clip(1.0 + 0.1 * jax.random.normal(seeds[9], (D,), jnp.float32), 0.5, 1.5),
        "qkv_weight": noise(seeds[10], (D, QKV), D ** -0.5, 0.09375, ((0, 16), (1, 2))),
    }


def request_plan(grid_sizes, image_owner, requests):
    image_rows = grid_sizes[:, 0] * grid_sizes[:, 1]
    member = (image_owner[:, None] == jnp.arange(requests, dtype=jnp.int32)[None, :]).astype(jnp.int32)
    counts = lax.optimization_barrier(jnp.sum(image_rows[:, None] * member, axis=0)).astype(jnp.int32)
    starts = (jnp.cumsum(counts) - counts).astype(jnp.int32)
    return (counts, starts)

def rope_tables(count):
    half_size = HEAD // 2
    exponent = jnp.arange(half_size, dtype=jnp.float32) * (2.0 / HEAD)
    frequency = jnp.exp(-exponent * jnp.log(jnp.float32(500000.0)))
    angles = jnp.arange(count, dtype=jnp.float32)[:, None] * frequency[None, :]
    return (jnp.cos(angles), jnp.sin(angles))

def apply_rope(projected, cosine_table, sine_table):
    seq_rows = projected.shape[0]
    head_blocks = projected.reshape(seq_rows, -1, GROUP + 2, HEAD)
    turning = head_blocks[:, :, :GROUP + 1, :]
    first_half = turning[..., :HEAD // 2]
    second_half = turning[..., HEAD // 2:]
    cosine_wide = cosine_table[:, None, None, :]
    sine_wide = sine_table[:, None, None, :]
    turned = jnp.concatenate([first_half * cosine_wide - second_half * sine_wide, second_half * cosine_wide + first_half * sine_wide], axis=-1)
    head_blocks = jnp.concatenate([turned, head_blocks[:, :, GROUP + 1:, :]], axis=2)
    return head_blocks.reshape(seq_rows, -1)

def normalize(embedded, norm_gain):
    values = embedded.astype(jnp.float32)
    mean_square = lax.optimization_barrier(jnp.mean(values * values, axis=-1, keepdims=True))
    return (values * lax.rsqrt(mean_square + 1e-05) * norm_gain[None, :]).astype(jnp.bfloat16)

def reference(vit_context, vision_residual, out_weight, layer_scale, prompt, prompt_len, image_at, grid_sizes, image_owner, norm_gain, qkv_weight):
    block_width = D // N_TP

    def vision_block(block_item):
        context_rows, residual_rows = block_item
        merged_context = lax.optimization_barrier(jnp.mean(context_rows.astype(jnp.float32).reshape(MRG_DEV, 4, D), axis=1)).astype(jnp.bfloat16)
        merged_residual = lax.optimization_barrier(jnp.mean(residual_rows.astype(jnp.float32).reshape(MRG_DEV, 4, D), axis=1))
        running = jnp.zeros((MRG_DEV, D), jnp.float32)
        for part_index in range(N_TP):
            column_start = part_index * block_width
            block_term = jnp.dot(merged_context[:, column_start:column_start + block_width], out_weight[column_start:column_start + block_width, :], preferred_element_type=jnp.float32)
            rounded = lax.optimization_barrier(block_term.astype(jnp.bfloat16))
            running = running + rounded.astype(jnp.float32)
        return (merged_residual + layer_scale[None, :] * running).astype(jnp.bfloat16)
    merged_blocks = lax.map(vision_block, (vit_context.reshape(REQS, P_DEV, D), vision_residual.reshape(REQS, P_DEV, D)))
    merged = jnp.transpose(merged_blocks, (1, 0, 2)).reshape(MRG_DEV * REQS, D)
    padded = jnp.concatenate([merged, jnp.zeros((IMG_MAX, D), merged.dtype)], axis=0)
    counts, starts = request_plan(grid_sizes, image_owner, REQS)
    cosine_table, sine_table = rope_tables(SEQ)

    def one_request(request_item):
        prompt_rows, own_count, own_start, prompt_count, image_from = request_item
        image_rows = lax.dynamic_slice_in_dim(padded, own_start.astype(jnp.int32), IMG_MAX, 0)
        slot_index = jnp.arange(SEQ, dtype=jnp.int32)
        image_row = slot_index - image_from
        in_image = (image_row >= 0) & (image_row < own_count)
        is_live = slot_index < prompt_count + own_count
        from_prompt = is_live & jnp.logical_not(in_image)
        prompt_row = jnp.where(slot_index < image_from, slot_index, slot_index - own_count)
        image_choice = jnp.take(image_rows, jnp.clip(image_row, 0, IMG_MAX - 1).astype(jnp.int32), axis=0)
        prompt_choice = jnp.take(prompt_rows, jnp.clip(prompt_row, 0, PROMPT_MAX - 1).astype(jnp.int32), axis=0)
        embedded = jnp.where(in_image[:, None], image_choice, jnp.where(from_prompt[:, None], prompt_choice, jnp.zeros_like(prompt_choice)))
        normed = normalize(embedded, norm_gain)
        projected = jnp.dot(normed, qkv_weight, preferred_element_type=jnp.float32)
        return apply_rope(projected, cosine_table, sine_table).astype(jnp.bfloat16)
    outputs = lax.map(one_request, (prompt, counts, starts, prompt_len, image_at))
    return outputs.reshape(REQS * SEQ, QKV)
```

```python
import jax
import jax.numpy as jnp
from jax import lax
from jax.sharding import PartitionSpec as P

HEAD = 128
GROUP = 4
IMG_MAX = 128


def request_plan(grid_sizes, image_owner, requests):
    image_rows = grid_sizes[:, 0] * grid_sizes[:, 1]
    member = (image_owner[:, None] == jnp.arange(requests, dtype=jnp.int32)[None, :]).astype(
        jnp.int32
    )
    counts = jnp.sum(image_rows[:, None] * member, axis=0)
    starts = jnp.cumsum(counts) - counts
    return (counts, starts)


def rope_tables(count):
    half_size = HEAD // 2
    exponent = jnp.arange(half_size, dtype=jnp.float32) * (2.0 / HEAD)
    frequency = jnp.exp(-exponent * jnp.log(jnp.float32(500000.0)))
    angles = jnp.arange(count, dtype=jnp.float32)[:, None] * frequency[None, :]
    return (jnp.cos(angles), jnp.sin(angles))


def apply_rope(projected, cosine_table, sine_table):
    seq_rows = projected.shape[0]
    head_blocks = projected.reshape(seq_rows, -1, GROUP + 2, HEAD)
    turning = head_blocks[:, :, : GROUP + 1, :]
    first_half = turning[..., : HEAD // 2]
    second_half = turning[..., HEAD // 2 :]
    cosine_wide = cosine_table[:, None, None, :]
    sine_wide = sine_table[:, None, None, :]
    turned = jnp.concatenate(
        [
            first_half * cosine_wide - second_half * sine_wide,
            second_half * cosine_wide + first_half * sine_wide,
        ],
        axis=-1,
    )
    head_blocks = jnp.concatenate([turned, head_blocks[:, :, GROUP + 1 :, :]], axis=2)
    return head_blocks.reshape(seq_rows, -1)


def shards(
    vit_context,
    vision_residual,
    out_weight,
    layer_scale,
    prompt,
    prompt_len,
    image_at,
    grid_sizes,
    image_owner,
    norm_gain,
    qkv_weight,
):
    requests = lax.axis_size("req")
    device_index = lax.axis_index("req")
    tp_index = lax.axis_index("tp")
    feature_width = vit_context.shape[1]
    plane = qkv_weight.shape[1] // ((GROUP + 2) * HEAD)
    depth = requests // plane
    in_plane = [[d * plane + i for i in range(plane)] for d in range(depth)]
    in_depth = [[d * plane + i for d in range(depth)] for i in range(plane)]
    weight_rows = qkv_weight.shape[0]
    weight_parts = jnp.swapaxes(qkv_weight.reshape(weight_rows, plane, -1), 0, 1)
    weight_parts = lax.all_to_all(
        weight_parts, "req", split_axis=0, concat_axis=0, axis_index_groups=in_plane, tiled=True
    )
    decoder_weight = lax.all_gather(
        weight_parts.reshape(plane * weight_rows, -1),
        "req",
        axis=0,
        axis_index_groups=in_depth,
        tiled=True,
    )
    merged_context = jnp.mean(
        vit_context.astype(jnp.float32).reshape(-1, 4, feature_width), axis=1
    ).astype(jnp.bfloat16)
    merged_residual = jnp.mean(
        vision_residual.astype(jnp.float32).reshape(-1, 4, feature_width), axis=1
    )
    partial_value = jnp.dot(
        lax.all_gather(merged_context, "req", axis=0, axis_index_groups=in_depth, tiled=True),
        lax.all_gather(out_weight, "req", axis=1, axis_index_groups=in_plane, tiled=True),
        preferred_element_type=jnp.float32,
    )
    returned = lax.all_to_all(
        partial_value.astype(jnp.bfloat16).reshape(depth, merged_context.shape[0], -1),
        "req",
        split_axis=0,
        concat_axis=0,
        axis_index_groups=in_depth,
        tiled=True,
    )
    returned = jnp.swapaxes(returned, 0, 1).reshape(merged_context.shape[0], -1)
    summed = lax.psum(returned, "tp").astype(jnp.float32)
    own_share = lax.dynamic_slice_in_dim(summed, tp_index * feature_width, feature_width, 1)
    merged = (merged_residual + layer_scale[None, :] * own_share).astype(jnp.bfloat16)
    merged_count = merged.shape[0]
    counts, starts = request_plan(grid_sizes, image_owner, requests)
    request_ends = starts + counts
    capacity = (IMG_MAX + requests - 1) // requests
    request_ids = jnp.arange(requests, dtype=jnp.int32)
    group_index = jnp.arange(merged_count, dtype=jnp.int32) * requests + device_index
    destination = jnp.sum((request_ends[None, :] <= group_index[:, None]).astype(jnp.int32), axis=1)
    owned_start = jnp.sum(
        jnp.where(destination[:, None] == request_ids[None, :], starts[None, :], 0), axis=1
    )
    target = destination * capacity + (group_index - owned_start) // requests
    usable = destination < requests
    send_slots = jnp.arange(requests * capacity, dtype=jnp.int32)
    placing = ((send_slots[:, None] == target[None, :]) & usable[None, :]).astype(jnp.bfloat16)
    outgoing = jnp.dot(placing, merged, preferred_element_type=jnp.float32).astype(jnp.bfloat16)
    arrived = lax.all_to_all(
        outgoing.reshape(requests, capacity, feature_width),
        "req",
        split_axis=0,
        concat_axis=0,
        tiled=True,
    )
    arrived = arrived.reshape(requests * capacity, feature_width)
    own_request = request_ids == device_index
    own_count = jnp.sum(jnp.where(own_request, counts, 0))
    own_start = jnp.sum(jnp.where(own_request, starts, 0))
    image_from = image_at[0]
    prompt_count = prompt_len[0]
    seq_slots = prompt.shape[1] + IMG_MAX
    slot_index = jnp.arange(seq_slots, dtype=jnp.int32)
    image_row = slot_index - image_from
    in_image = (image_row >= 0) & (image_row < own_count)
    is_live = slot_index < prompt_count + own_count
    from_prompt = is_live & jnp.logical_not(in_image)
    flat_index = (own_start + image_row) % requests * capacity + image_row // requests
    image_pick = ((flat_index[:, None] == send_slots[None, :]) & in_image[:, None]).astype(
        jnp.bfloat16
    )
    prompt_row = jnp.where(slot_index < image_from, slot_index, slot_index - own_count)
    prompt_ids = jnp.arange(prompt.shape[1], dtype=jnp.int32)
    prompt_pick = ((prompt_row[:, None] == prompt_ids[None, :]) & from_prompt[:, None]).astype(
        jnp.bfloat16
    )
    embedded = (
        jnp.dot(image_pick, arrived, preferred_element_type=jnp.float32)
        + jnp.dot(prompt_pick, prompt[0], preferred_element_type=jnp.float32)
    ).astype(jnp.bfloat16)
    values = embedded.astype(jnp.float32)
    square_sum = lax.psum(jnp.sum(values * values, axis=-1, keepdims=True), "tp")
    mean_square = square_sum / (feature_width * lax.axis_size("tp"))
    own_gain = lax.dynamic_slice_in_dim(norm_gain, tp_index * feature_width, feature_width, 0)
    normed = (values * lax.rsqrt(mean_square + 1e-05) * own_gain[None, :]).astype(jnp.bfloat16)
    normed = lax.all_gather(normed, "req", axis=0, axis_index_groups=in_plane, tiled=True)
    normed = lax.all_gather(normed, "tp", axis=1, tiled=True)
    projected = jnp.dot(normed, decoder_weight, preferred_element_type=jnp.float32)
    cosine_table, sine_table = rope_tables(seq_slots)
    cosine_table = jnp.tile(cosine_table, (plane, 1))
    sine_table = jnp.tile(sine_table, (plane, 1))
    turned = apply_rope(projected, cosine_table, sine_table).astype(jnp.bfloat16)
    turned = lax.all_to_all(
        turned.reshape(plane, seq_slots, -1),
        "req",
        split_axis=0,
        concat_axis=0,
        axis_index_groups=in_plane,
        tiled=True,
    )
    return jnp.swapaxes(turned, 0, 1).reshape(seq_slots, -1)


def solution(mesh):
    in_specs = (
        P("req", "tp"),
        P("req", "tp"),
        P("tp", "req"),
        P("tp"),
        P("req", None, "tp"),
        P("req"),
        P("req"),
        P(),
        P(),
        P(),
        P("req", "tp"),
    )
    out_specs = P("req", "tp")
    return jax.shard_map(shards, mesh=mesh, in_specs=in_specs, out_specs=out_specs, check_vma=False)
```

```python
import functools

import jax
import jax.numpy as jnp
from jax import lax
from jax.experimental import pallas as pl
from jax.experimental.pallas import tpu as pltpu
from jax.sharding import PartitionSpec as P

HEAD = 128
GROUP = 4
IMG_MAX = 128


def request_plan(grid_sizes, image_owner, requests):
    image_rows = grid_sizes[:, 0] * grid_sizes[:, 1]
    member = (image_owner[:, None] == jnp.arange(requests, dtype=jnp.int32)[None, :]).astype(
        jnp.int32
    )
    counts = jnp.sum(image_rows[:, None] * member, axis=0)
    starts = jnp.cumsum(counts) - counts
    return (counts, starts)


def rope_tables(count):
    half_size = HEAD // 2
    exponent = jnp.arange(half_size, dtype=jnp.float32) * (2.0 / HEAD)
    frequency = jnp.exp(-exponent * jnp.log(jnp.float32(500000.0)))
    angles = jnp.arange(count, dtype=jnp.float32)[:, None] * frequency[None, :]
    return (jnp.cos(angles), jnp.sin(angles))


def apply_rope(projected, cosine_table, sine_table):
    seq_rows = projected.shape[0]
    head_blocks = projected.reshape(seq_rows, -1, GROUP + 2, HEAD)
    turning = head_blocks[:, :, : GROUP + 1, :]
    first_half = turning[..., : HEAD // 2]
    second_half = turning[..., HEAD // 2 :]
    cosine_wide = cosine_table[:, None, None, :]
    sine_wide = sine_table[:, None, None, :]
    turned = jnp.concatenate(
        [
            first_half * cosine_wide - second_half * sine_wide,
            second_half * cosine_wide + first_half * sine_wide,
        ],
        axis=-1,
    )
    head_blocks = jnp.concatenate([turned, head_blocks[:, :, GROUP + 1 :, :]], axis=2)
    return head_blocks.reshape(seq_rows, -1)


def collective_shards(
    vit_context,
    vision_residual,
    out_weight,
    layer_scale,
    prompt,
    prompt_len,
    image_at,
    grid_sizes,
    image_owner,
    norm_gain,
    qkv_weight,
):
    requests = lax.axis_size("req")
    device_index = lax.axis_index("req")
    tp_index = lax.axis_index("tp")
    feature_width = vit_context.shape[1]
    plane = qkv_weight.shape[1] // ((GROUP + 2) * HEAD)
    depth = requests // plane
    in_plane = [[d * plane + i for i in range(plane)] for d in range(depth)]
    in_depth = [[d * plane + i for d in range(depth)] for i in range(plane)]
    weight_rows = qkv_weight.shape[0]
    weight_parts = jnp.swapaxes(qkv_weight.reshape(weight_rows, plane, -1), 0, 1)
    weight_parts = lax.all_to_all(
        weight_parts, "req", split_axis=0, concat_axis=0, axis_index_groups=in_plane, tiled=True
    )
    decoder_weight = lax.all_gather(
        weight_parts.reshape(plane * weight_rows, -1),
        "req",
        axis=0,
        axis_index_groups=in_depth,
        tiled=True,
    )
    merged_context = jnp.mean(
        vit_context.astype(jnp.float32).reshape(-1, 4, feature_width), axis=1
    ).astype(jnp.bfloat16)
    merged_residual = jnp.mean(
        vision_residual.astype(jnp.float32).reshape(-1, 4, feature_width), axis=1
    )
    partial_value = jnp.dot(
        lax.all_gather(merged_context, "req", axis=0, axis_index_groups=in_depth, tiled=True),
        lax.all_gather(out_weight, "req", axis=1, axis_index_groups=in_plane, tiled=True),
        preferred_element_type=jnp.float32,
    )
    returned = lax.all_to_all(
        partial_value.astype(jnp.bfloat16).reshape(depth, merged_context.shape[0], -1),
        "req",
        split_axis=0,
        concat_axis=0,
        axis_index_groups=in_depth,
        tiled=True,
    )
    returned = jnp.swapaxes(returned, 0, 1).reshape(merged_context.shape[0], -1)
    summed = lax.psum(returned, "tp").astype(jnp.float32)
    own_share = lax.dynamic_slice_in_dim(summed, tp_index * feature_width, feature_width, 1)
    merged = (merged_residual + layer_scale[None, :] * own_share).astype(jnp.bfloat16)
    merged_count = merged.shape[0]
    counts, starts = request_plan(grid_sizes, image_owner, requests)
    request_ends = starts + counts
    capacity = (IMG_MAX + requests - 1) // requests
    request_ids = jnp.arange(requests, dtype=jnp.int32)
    group_index = jnp.arange(merged_count, dtype=jnp.int32) * requests + device_index
    destination = jnp.sum((request_ends[None, :] <= group_index[:, None]).astype(jnp.int32), axis=1)
    owned_start = jnp.sum(
        jnp.where(destination[:, None] == request_ids[None, :], starts[None, :], 0), axis=1
    )
    target = destination * capacity + (group_index - owned_start) // requests
    usable = destination < requests
    send_slots = jnp.arange(requests * capacity, dtype=jnp.int32)
    placing = ((send_slots[:, None] == target[None, :]) & usable[None, :]).astype(jnp.bfloat16)
    outgoing = jnp.dot(placing, merged, preferred_element_type=jnp.float32).astype(jnp.bfloat16)
    arrived = lax.all_to_all(
        outgoing.reshape(requests, capacity, feature_width),
        "req",
        split_axis=0,
        concat_axis=0,
        tiled=True,
    )
    arrived = arrived.reshape(requests * capacity, feature_width)
    own_request = request_ids == device_index
    own_count = jnp.sum(jnp.where(own_request, counts, 0))
    own_start = jnp.sum(jnp.where(own_request, starts, 0))
    image_from = image_at[0]
    prompt_count = prompt_len[0]
    seq_slots = prompt.shape[1] + IMG_MAX
    slot_index = jnp.arange(seq_slots, dtype=jnp.int32)
    image_row = slot_index - image_from
    in_image = (image_row >= 0) & (image_row < own_count)
    is_live = slot_index < prompt_count + own_count
    from_prompt = is_live & jnp.logical_not(in_image)
    flat_index = (own_start + image_row) % requests * capacity + image_row // requests
    image_pick = ((flat_index[:, None] == send_slots[None, :]) & in_image[:, None]).astype(
        jnp.bfloat16
    )
    prompt_row = jnp.where(slot_index < image_from, slot_index, slot_index - own_count)
    prompt_ids = jnp.arange(prompt.shape[1], dtype=jnp.int32)
    prompt_pick = ((prompt_row[:, None] == prompt_ids[None, :]) & from_prompt[:, None]).astype(
        jnp.bfloat16
    )
    embedded = (
        jnp.dot(image_pick, arrived, preferred_element_type=jnp.float32)
        + jnp.dot(prompt_pick, prompt[0], preferred_element_type=jnp.float32)
    ).astype(jnp.bfloat16)
    values = embedded.astype(jnp.float32)
    square_sum = lax.psum(jnp.sum(values * values, axis=-1, keepdims=True), "tp")
    mean_square = square_sum / (feature_width * lax.axis_size("tp"))
    own_gain = lax.dynamic_slice_in_dim(norm_gain, tp_index * feature_width, feature_width, 0)
    normed = (values * lax.rsqrt(mean_square + 1e-05) * own_gain[None, :]).astype(jnp.bfloat16)
    normed = lax.all_gather(normed, "req", axis=0, axis_index_groups=in_plane, tiled=True)
    normed = lax.all_gather(normed, "tp", axis=1, tiled=True)
    projected = jnp.dot(normed, decoder_weight, preferred_element_type=jnp.float32)
    cosine_table, sine_table = rope_tables(seq_slots)
    cosine_table = jnp.tile(cosine_table, (plane, 1))
    sine_table = jnp.tile(sine_table, (plane, 1))
    turned = apply_rope(projected, cosine_table, sine_table).astype(jnp.bfloat16)
    turned = lax.all_to_all(
        turned.reshape(plane, seq_slots, -1),
        "req",
        split_axis=0,
        concat_axis=0,
        axis_index_groups=in_plane,
        tiled=True,
    )
    return jnp.swapaxes(turned, 0, 1).reshape(seq_slots, -1)


MESH = pl.DeviceIdType.MESH
BF16 = jnp.bfloat16
F32 = jnp.float32


def dot(a, b):
    return jnp.dot(a, b, preferred_element_type=F32)


def fused_kernel(
    dims,
    context,
    residual,
    out_weight,
    scale,
    prompt,
    gain,
    qkv_weight,
    averaging,
    place_left,
    place_right,
    pick_left,
    pick_right,
    prompt_pick,
    cosine,
    sine,
    out,
    slab,
    out_slab,
    blocks,
    partials,
    returned,
    mean_residual,
    merged,
    outgoing,
    arrived,
    embedded,
    squares,
    normed,
    total,
    turned,
    slab_in_send,
    slab_in_recv,
    slab_local,
    slab_send,
    slab_recv,
    out_slab_send,
    out_slab_recv,
    out_slab_local,
    block_send,
    block_recv,
    partial_send,
    partial_recv,
    place_send,
    place_recv,
    square_send,
    square_recv,
    normed_send,
    normed_recv,
    cross_send,
    turned_send,
    turned_recv,
    turned_local,
):
    requests, cores, plane, depth = dims
    req = lax.axis_index("req")
    core = lax.axis_index("tp")
    level = req // plane
    spot = req % plane
    sibling = 1 - core
    rows = blocks.shape[1]
    width = blocks.shape[2]
    depth_rows = qkv_weight.shape[0]
    share = slab.shape[-1]
    columns = out_weight.shape[1]
    seq = out.shape[0]
    half = width // 2
    held = depth // cores
    others = [
        ((spot // 2 + ry) % 2) * 2 + (spot % 2 + rx) % 2 for ry, rx in ((0, 1), (1, 0), (1, 1))
    ]

    def remote(src, dst, send, recv, to_req, to_core):
        return pltpu.make_async_remote_copy(
            src_ref=src,
            dst_ref=dst,
            send_sem=send,
            recv_sem=recv,
            device_id=(to_req, to_core),
            device_id_type=MESH,
        )

    def arrive(dst, recv):
        remote(dst, dst, slab_local, recv, req, sibling).wait_recv()

    barrier = pltpu.get_barrier_semaphore()
    count = requests * cores

    @pl.loop(1, count)
    def _(offset):
        at = (req * cores + core + offset) % count
        pl.semaphore_signal(
            barrier, inc=1, device_id=(at // cores, at % cores), device_id_type=MESH
        )

    pl.semaphore_wait(barrier, count - 1)

    out_sends = []
    for i, other in enumerate(others):
        out_sends.append(
            remote(
                out_weight,
                out_slab.at[spot],
                out_slab_send.at[i],
                out_slab_recv.at[spot],
                level * plane + other,
                core,
            )
        )
        out_sends[-1].start()
    out_own = pltpu.make_async_copy(out_weight, out_slab.at[spot], out_slab_local)
    out_own.start()

    for i in range(width // 512):
        cols = slice(i * 512, (i + 1) * 512)
        blocks[level, :, cols] = dot(averaging[...], context[:, cols]).astype(BF16)

    def pass_on(buffer, send, recv, hop, first):
        if hop > 1:

            @pl.when(level - (hop - 1) >= 0)
            def _():
                arrive(buffer.at[level - (hop - 1)], recv.at[level - (hop - 1)])

            @pl.when(level + (hop - 1) < depth)
            def _():
                arrive(buffer.at[level + (hop - 1)], recv.at[level + (hop - 1)])

        if hop == depth:
            return

        @pl.when((level - (hop - 1) >= 0) & (level + 1 < depth))
        def _():
            at = level - (hop - 1)
            remote(
                buffer.at[at], buffer.at[at], send.at[hop - 1, 0], recv.at[at], req + plane, core
            ).start()

        @pl.when((level + (hop - 1) < depth) & (level - 1 >= 0))
        def _():
            at = level + (hop - 1)
            remote(
                buffer.at[at], buffer.at[at], send.at[hop - 1, 1], recv.at[at], req - plane, core
            ).start()

    def passed(buffer, send, recv):
        for hop in range(1, depth):

            @pl.when((level - (hop - 1) >= 0) & (level + 1 < depth))
            def _():
                at = level - (hop - 1)
                remote(
                    buffer.at[at], buffer.at[at], send.at[hop - 1, 0], recv.at[at], req, sibling
                ).wait_send()

            @pl.when((level + (hop - 1) < depth) & (level - 1 >= 0))
            def _():
                at = level + (hop - 1)
                remote(
                    buffer.at[at], buffer.at[at], send.at[hop - 1, 1], recv.at[at], req, sibling
                ).wait_send()

    pass_on(blocks, block_send, block_recv, 1, True)

    slab_sends = []
    for i, other in enumerate(others):
        at = pl.multiple_of(other * share, share)
        slab_sends.append(
            remote(
                qkv_weight.at[:, pl.ds(at, share)],
                slab.at[level, spot],
                slab_in_send.at[i],
                slab_in_recv.at[spot],
                level * plane + other,
                core,
            )
        )
        slab_sends[-1].start()
    slab_own = pltpu.make_async_copy(
        qkv_weight.at[:, pl.ds(pl.multiple_of(spot * share, share), share)],
        slab.at[level, spot],
        slab_local,
    )
    slab_own.start()

    for i in range(width // 512):
        cols = slice(i * 512, (i + 1) * 512)
        mean_residual[:, cols] = dot(averaging[...], residual[:, cols])

    for hop in range(2, depth + 1):
        pass_on(blocks, block_send, block_recv, hop, True)
    passed(blocks, block_send, block_recv)

    slab_own.wait()
    for other in others:
        arrive(slab.at[level, other], slab_in_recv.at[other])
    pass_on(slab, slab_send, slab_recv, 1, False)

    out_own.wait()
    for other in others:
        arrive(out_slab.at[other], out_slab_recv.at[other])

    owner_core = level // held
    lane = level % held

    @pl.loop(0, depth)
    def _(step):
        target = (level + 1 + step) % depth
        for i in range(plane):
            partials[target, :, i * columns : (i + 1) * columns] = dot(
                blocks[target], out_slab[i]
            ).astype(BF16)
        own = (target == level) & (owner_core == core)

        @pl.when(own)
        def _():
            pltpu.make_async_copy(
                partials.at[target], returned.at[lane, core], partial_recv.at[lane, core]
            ).start()

        @pl.when(jnp.logical_not(own))
        def _():
            remote(
                partials.at[target],
                returned.at[lane, core],
                partial_send.at[target],
                partial_recv.at[lane, core],
                target * plane + spot,
                owner_core,
            ).start()

    for i in range(held):
        for j in range(cores):
            arrive(returned.at[i, j], partial_recv.at[i, j])
    for i in range(held):
        cols = slice(i * half, (i + 1) * half)
        added = returned[i, 0].astype(F32)
        for j in range(1, cores):
            added = added + returned[i, j].astype(F32)
        merged[:, cols] = (mean_residual[:, cols] + scale[:, cols] * added).astype(BF16)

    placed = dot(place_left[...], merged[:, :half]) + dot(place_right[...], merged[:, half:])
    outgoing[...] = placed.astype(BF16).reshape(outgoing.shape)

    @pl.loop(1, requests)
    def _(offset):
        to = (req + offset) % requests
        remote(
            outgoing.at[to], arrived.at[req], place_send.at[to], place_recv.at[req], to, core
        ).start()

    place_own = pltpu.make_async_copy(outgoing.at[req], arrived.at[req], place_send.at[req])
    place_own.start()
    for i in range(2):
        cols = slice(i * half, (i + 1) * half)
        embedded[:, cols] = dot(prompt_pick[...], prompt[:, cols])
    place_own.wait()

    @pl.loop(1, requests)
    def _(offset):
        source = (req + offset) % requests
        arrive(arrived.at[source], place_recv.at[source])

    square_sum = jnp.zeros((seq, 1), F32)
    for i, pick in enumerate((pick_left, pick_right)):
        cols = slice(i * half, (i + 1) * half)
        images = arrived[...].reshape(arrived.shape[0] * arrived.shape[1], half)
        values = embedded[:, cols] + dot(pick[...], images)
        embedded[:, cols] = values
        square_sum = square_sum + jnp.sum(values * values, axis=-1, keepdims=True)
    squares[0] = jnp.broadcast_to(square_sum, squares.shape[1:])
    square_copy = remote(squares.at[0], squares.at[1], square_send, square_recv, req, sibling)
    square_copy.start()
    square_copy.wait()
    mean_square = (squares[0, :, :1] + squares[1, :, :1]) / (width * cores)
    factor = lax.rsqrt(mean_square + 1e-05)
    for i in range(2):
        cols = slice(i * half, (i + 1) * half)
        normed[spot, core, :, cols] = (embedded[:, cols] * factor * gain[:, cols]).astype(BF16)

    normed_sends = []
    for i, other in enumerate(others):
        normed_sends.append(
            remote(
                normed.at[spot, core],
                normed.at[spot, core],
                normed_send.at[i],
                normed_recv.at[spot, core],
                level * plane + other,
                core,
            )
        )
        normed_sends[-1].start()

    def cross(place, i):
        copy = remote(
            normed.at[place, core],
            normed.at[place, core],
            cross_send.at[i],
            normed_recv.at[place, core],
            req,
            sibling,
        )
        copy.start()
        normed_sends.append(copy)

    cross(spot, 0)
    pass_on(slab, slab_send, slab_recv, 2, False)
    for hop in range(3, depth):
        pass_on(slab, slab_send, slab_recv, hop, False)
    for i, other in enumerate(others):
        arrive(normed.at[other, core], normed_recv.at[other, core])
        cross(other, i + 1)
    for place in [spot] + others:
        arrive(normed.at[place, sibling], normed_recv.at[place, sibling])

    tile = 256
    level_rows = plane * depth_rows

    def multiply(at, first):
        part = at // held
        base = pl.multiple_of((at % held) * level_rows, level_rows)

        @pl.loop(0, plane)
        def _(place):
            a = normed[place, part, :, pl.ds(base, level_rows)]
            for n in range(share // tile):
                cols = slice(n * tile, (n + 1) * tile)
                b = slab[at, :, :, cols].reshape(level_rows, tile)
                if first:
                    total[place, :, cols] = dot(a, b)
                else:
                    total[place, :, cols] += dot(a, b)

    multiply(level, True)
    for hop in range(1, depth):
        if hop == depth - 1:
            pass_on(slab, slab_send, slab_recv, depth, False)

        @pl.when(level - hop >= 0)
        def _():
            multiply(level - hop, False)

        @pl.when(level + hop < depth)
        def _():
            multiply(level + hop, False)

    turned_sends = []
    here = pl.ds(pl.multiple_of(spot * share, share), share)
    for i, place in enumerate(others + [spot]):
        for head in range(share // HEAD):
            cols = slice(head * HEAD, (head + 1) * HEAD)
            values = total[place, :, cols]
            if head <= GROUP:
                values = values * cosine[...] + pltpu.roll(values, HEAD // 2, 1) * sine[...]
            turned[place, :, cols] = values.astype(BF16)
        if i < len(others):
            turned_sends.append(
                remote(
                    turned.at[place],
                    out.at[:, here],
                    turned_send.at[i],
                    turned_recv.at[spot],
                    level * plane + place,
                    core,
                )
            )
            turned_sends[-1].start()
    turned_own = pltpu.make_async_copy(turned.at[spot], out.at[:, here], turned_local)
    turned_own.start()

    for copy in out_sends + slab_sends + normed_sends:
        copy.wait_send()
    passed(slab, slab_send, slab_recv)

    @pl.loop(0, depth)
    def _(target):
        @pl.when(jnp.logical_not((target == level) & (owner_core == core)))
        def _():
            remote(
                partials.at[target],
                returned.at[lane, core],
                partial_send.at[target],
                partial_recv.at[lane, core],
                req,
                sibling,
            ).wait_send()

    @pl.loop(1, requests)
    def _(offset):
        to = (req + offset) % requests
        remote(
            outgoing.at[to], arrived.at[req], place_send.at[to], place_recv.at[req], req, sibling
        ).wait_send()

    for copy in turned_sends:
        copy.wait_send()
    turned_own.wait()
    for other in others:
        there = pl.ds(pl.multiple_of(other * share, share), share)
        arrive(out.at[:, there], turned_recv.at[other])


def fused_shards(
    vit_context,
    vision_residual,
    out_weight,
    layer_scale,
    prompt,
    prompt_len,
    image_at,
    grid_sizes,
    image_owner,
    norm_gain,
    qkv_weight,
):
    requests = lax.axis_size("req")
    cores = lax.axis_size("tp")
    device_index = lax.axis_index("req")
    tp_index = lax.axis_index("tp")
    patches, width = vit_context.shape
    rows = patches // 4
    share = (GROUP + 2) * HEAD
    plane = qkv_weight.shape[1] // share
    depth = requests // plane
    seq_slots = prompt.shape[1] + IMG_MAX

    averaging = jnp.where(
        jnp.arange(patches)[None, :] // 4 == jnp.arange(rows)[:, None], 0.25, 0.0
    ).astype(BF16)
    counts, starts = request_plan(grid_sizes, image_owner, requests)
    request_ends = starts + counts
    capacity = (IMG_MAX + requests - 1) // requests
    request_ids = jnp.arange(requests, dtype=jnp.int32)
    group_index = jnp.arange(rows, dtype=jnp.int32) * requests + device_index
    destination = jnp.sum((request_ends[None, :] <= group_index[:, None]).astype(jnp.int32), axis=1)
    owned_start = jnp.sum(
        jnp.where(destination[:, None] == request_ids[None, :], starts[None, :], 0), axis=1
    )
    target = destination * 2 * capacity + (group_index - owned_start) // requests
    usable = destination < requests
    slots = jnp.arange(requests * 2 * capacity, dtype=jnp.int32)
    place_left = ((slots[:, None] == target[None, :]) & usable[None, :]).astype(BF16)
    place_right = ((slots[:, None] == target[None, :] + capacity) & usable[None, :]).astype(BF16)
    own_request = request_ids == device_index
    own_count = jnp.sum(jnp.where(own_request, counts, 0))
    own_start = jnp.sum(jnp.where(own_request, starts, 0))
    image_from = image_at[0]
    prompt_count = prompt_len[0]
    slot_index = jnp.arange(seq_slots, dtype=jnp.int32)
    image_row = slot_index - image_from
    in_image = (image_row >= 0) & (image_row < own_count)
    is_live = slot_index < prompt_count + own_count
    from_prompt = is_live & jnp.logical_not(in_image)
    flat_index = (own_start + image_row) % requests * 2 * capacity + image_row // requests
    pick_left = ((flat_index[:, None] == slots[None, :]) & in_image[:, None]).astype(BF16)
    pick_right = ((flat_index[:, None] + capacity == slots[None, :]) & in_image[:, None]).astype(
        BF16
    )
    prompt_row = jnp.where(slot_index < image_from, slot_index, slot_index - own_count)
    prompt_ids = jnp.arange(prompt.shape[1], dtype=jnp.int32)
    prompt_pick = ((prompt_row[:, None] == prompt_ids[None, :]) & from_prompt[:, None]).astype(BF16)
    own_gain = lax.dynamic_slice_in_dim(norm_gain, tp_index * width, width, 0)
    cosine_table, sine_table = rope_tables(seq_slots)
    cosine = jnp.concatenate([cosine_table, cosine_table], axis=1)
    sine = jnp.concatenate([-sine_table, sine_table], axis=1)

    vmem = pl.BlockSpec(memory_space=pltpu.VMEM)
    anywhere = pl.BlockSpec(memory_space=pl.ANY)
    dma = pltpu.SemaphoreType.DMA
    columns = out_weight.shape[1]
    half = width // 2
    return pl.pallas_call(
        functools.partial(fused_kernel, (requests, cores, plane, depth)),
        out_shape=jax.ShapeDtypeStruct((seq_slots, qkv_weight.shape[1]), BF16),
        in_specs=[vmem, vmem, anywhere, vmem, vmem, vmem, anywhere] + [vmem] * 8,
        out_specs=anywhere,
        scratch_shapes=[
            pltpu.VMEM((depth, plane, qkv_weight.shape[0], share), BF16),
            pltpu.VMEM((plane, width, columns), BF16),
            pltpu.VMEM((depth, rows, width), BF16),
            pltpu.VMEM((depth, rows, plane * columns), BF16),
            pltpu.VMEM((depth // cores, cores, rows, plane * columns), BF16),
            pltpu.VMEM((rows, width), F32),
            pltpu.VMEM((rows, width), BF16),
            pltpu.VMEM((requests, 2 * capacity, half), BF16),
            pltpu.VMEM((requests, 2 * capacity, half), BF16),
            pltpu.VMEM((seq_slots, width), F32),
            pltpu.VMEM((2, seq_slots, 128), F32),
            pltpu.VMEM((plane, cores, seq_slots, width), BF16),
            pltpu.VMEM((plane, seq_slots, share), F32),
            pltpu.VMEM((plane, seq_slots, share), BF16),
            dma((plane,)),
            dma((plane,)),
            dma,
            dma((depth, 2)),
            dma((depth,)),
            dma((plane,)),
            dma((plane,)),
            dma,
            dma((depth, 2)),
            dma((depth,)),
            dma((depth,)),
            dma((depth // cores, cores)),
            dma((requests,)),
            dma((requests,)),
            dma,
            dma,
            dma((plane,)),
            dma((plane, cores)),
            dma((plane,)),
            dma((plane,)),
            dma((plane,)),
            dma,
        ],
        compiler_params=pltpu.CompilerParams(
            collective_id=0, has_side_effects=True, vmem_limit_bytes=58 * 1024 * 1024
        ),
        cost_estimate=pl.CostEstimate(
            flops=30 * 10**9, bytes_accessed=20 * 2**20, transcendentals=0
        ),
    )(
        vit_context,
        vision_residual,
        out_weight,
        layer_scale[None, :],
        prompt[0],
        own_gain[None, :],
        qkv_weight,
        averaging,
        place_left,
        place_right,
        pick_left,
        pick_right,
        prompt_pick,
        cosine,
        sine,
    )


def solution(mesh):
    requests, cores = mesh.shape["req"], mesh.shape["tp"]

    def shards(*arrays):
        patches, width = arrays[0].shape
        plane = arrays[-1].shape[1] // ((GROUP + 2) * HEAD)
        fits = (
            cores == 2
            and plane == 4
            and requests // plane % cores == 0
            and arrays[2].shape[1] * requests == width * cores
            and arrays[2].shape[1] % 128 == 0
            and IMG_MAX % requests == 0
            and (IMG_MAX // requests) % 8 == 0
        )
        return (fused_shards if fits else collective_shards)(*arrays)

    in_specs = (
        P("req", "tp"),
        P("req", "tp"),
        P("tp", "req"),
        P("tp"),
        P("req", None, "tp"),
        P("req"),
        P("req"),
        P(),
        P(),
        P(),
        P("req", "tp"),
    )
    out_specs = P("req", "tp")
    return jax.shard_map(shards, mesh=mesh, in_specs=in_specs, out_specs=out_specs, check_vma=False)
```

```python
import functools

import jax
import jax.numpy as jnp
from jax import lax
from jax.experimental import pallas as pl
from jax.experimental.pallas import tpu as pltpu
from jax.sharding import PartitionSpec as P

HEAD = 128
GROUP = 4
IMG_MAX = 128


def request_plan(grid_sizes, image_owner, requests):
    image_rows = grid_sizes[:, 0] * grid_sizes[:, 1]
    member = (image_owner[:, None] == jnp.arange(requests, dtype=jnp.int32)[None, :]).astype(
        jnp.int32
    )
    counts = jnp.sum(image_rows[:, None] * member, axis=0)
    starts = jnp.cumsum(counts) - counts
    return (counts, starts)


def rope_tables(count):
    half_size = HEAD // 2
    exponent = jnp.arange(half_size, dtype=jnp.float32) * (2.0 / HEAD)
    frequency = jnp.exp(-exponent * jnp.log(jnp.float32(500000.0)))
    angles = jnp.arange(count, dtype=jnp.float32)[:, None] * frequency[None, :]
    return (jnp.cos(angles), jnp.sin(angles))


def apply_rope(projected, cosine_table, sine_table):
    seq_rows = projected.shape[0]
    head_blocks = projected.reshape(seq_rows, -1, GROUP + 2, HEAD)
    turning = head_blocks[:, :, : GROUP + 1, :]
    first_half = turning[..., : HEAD // 2]
    second_half = turning[..., HEAD // 2 :]
    cosine_wide = cosine_table[:, None, None, :]
    sine_wide = sine_table[:, None, None, :]
    turned = jnp.concatenate(
        [
            first_half * cosine_wide - second_half * sine_wide,
            second_half * cosine_wide + first_half * sine_wide,
        ],
        axis=-1,
    )
    head_blocks = jnp.concatenate([turned, head_blocks[:, :, GROUP + 1 :, :]], axis=2)
    return head_blocks.reshape(seq_rows, -1)


def collective_shards(
    vit_context,
    vision_residual,
    out_weight,
    layer_scale,
    prompt,
    prompt_len,
    image_at,
    grid_sizes,
    image_owner,
    norm_gain,
    qkv_weight,
):
    requests = lax.axis_size("req")
    device_index = lax.axis_index("req")
    tp_index = lax.axis_index("tp")
    feature_width = vit_context.shape[1]
    plane = qkv_weight.shape[1] // ((GROUP + 2) * HEAD)
    depth = requests // plane
    in_plane = [[d * plane + i for i in range(plane)] for d in range(depth)]
    in_depth = [[d * plane + i for d in range(depth)] for i in range(plane)]
    weight_rows = qkv_weight.shape[0]
    weight_parts = jnp.swapaxes(qkv_weight.reshape(weight_rows, plane, -1), 0, 1)
    weight_parts = lax.all_to_all(
        weight_parts, "req", split_axis=0, concat_axis=0, axis_index_groups=in_plane, tiled=True
    )
    decoder_weight = lax.all_gather(
        weight_parts.reshape(plane * weight_rows, -1),
        "req",
        axis=0,
        axis_index_groups=in_depth,
        tiled=True,
    )
    merged_context = jnp.mean(
        vit_context.astype(jnp.float32).reshape(-1, 4, feature_width), axis=1
    ).astype(jnp.bfloat16)
    merged_residual = jnp.mean(
        vision_residual.astype(jnp.float32).reshape(-1, 4, feature_width), axis=1
    )
    partial_value = jnp.dot(
        lax.all_gather(merged_context, "req", axis=0, axis_index_groups=in_depth, tiled=True),
        lax.all_gather(out_weight, "req", axis=1, axis_index_groups=in_plane, tiled=True),
        preferred_element_type=jnp.float32,
    )
    returned = lax.all_to_all(
        partial_value.astype(jnp.bfloat16).reshape(depth, merged_context.shape[0], -1),
        "req",
        split_axis=0,
        concat_axis=0,
        axis_index_groups=in_depth,
        tiled=True,
    )
    returned = jnp.swapaxes(returned, 0, 1).reshape(merged_context.shape[0], -1)
    summed = lax.psum(returned, "tp").astype(jnp.float32)
    own_share = lax.dynamic_slice_in_dim(summed, tp_index * feature_width, feature_width, 1)
    merged = (merged_residual + layer_scale[None, :] * own_share).astype(jnp.bfloat16)
    merged_count = merged.shape[0]
    counts, starts = request_plan(grid_sizes, image_owner, requests)
    request_ends = starts + counts
    capacity = (IMG_MAX + requests - 1) // requests
    request_ids = jnp.arange(requests, dtype=jnp.int32)
    group_index = jnp.arange(merged_count, dtype=jnp.int32) * requests + device_index
    destination = jnp.sum((request_ends[None, :] <= group_index[:, None]).astype(jnp.int32), axis=1)
    owned_start = jnp.sum(
        jnp.where(destination[:, None] == request_ids[None, :], starts[None, :], 0), axis=1
    )
    target = destination * capacity + (group_index - owned_start) // requests
    usable = destination < requests
    send_slots = jnp.arange(requests * capacity, dtype=jnp.int32)
    placing = ((send_slots[:, None] == target[None, :]) & usable[None, :]).astype(jnp.bfloat16)
    outgoing = jnp.dot(placing, merged, preferred_element_type=jnp.float32).astype(jnp.bfloat16)
    arrived = lax.all_to_all(
        outgoing.reshape(requests, capacity, feature_width),
        "req",
        split_axis=0,
        concat_axis=0,
        tiled=True,
    )
    arrived = arrived.reshape(requests * capacity, feature_width)
    own_request = request_ids == device_index
    own_count = jnp.sum(jnp.where(own_request, counts, 0))
    own_start = jnp.sum(jnp.where(own_request, starts, 0))
    image_from = image_at[0]
    prompt_count = prompt_len[0]
    seq_slots = prompt.shape[1] + IMG_MAX
    slot_index = jnp.arange(seq_slots, dtype=jnp.int32)
    image_row = slot_index - image_from
    in_image = (image_row >= 0) & (image_row < own_count)
    is_live = slot_index < prompt_count + own_count
    from_prompt = is_live & jnp.logical_not(in_image)
    flat_index = (own_start + image_row) % requests * capacity + image_row // requests
    image_pick = ((flat_index[:, None] == send_slots[None, :]) & in_image[:, None]).astype(
        jnp.bfloat16
    )
    prompt_row = jnp.where(slot_index < image_from, slot_index, slot_index - own_count)
    prompt_ids = jnp.arange(prompt.shape[1], dtype=jnp.int32)
    prompt_pick = ((prompt_row[:, None] == prompt_ids[None, :]) & from_prompt[:, None]).astype(
        jnp.bfloat16
    )
    embedded = (
        jnp.dot(image_pick, arrived, preferred_element_type=jnp.float32)
        + jnp.dot(prompt_pick, prompt[0], preferred_element_type=jnp.float32)
    ).astype(jnp.bfloat16)
    values = embedded.astype(jnp.float32)
    square_sum = lax.psum(jnp.sum(values * values, axis=-1, keepdims=True), "tp")
    mean_square = square_sum / (feature_width * lax.axis_size("tp"))
    own_gain = lax.dynamic_slice_in_dim(norm_gain, tp_index * feature_width, feature_width, 0)
    normed = (values * lax.rsqrt(mean_square + 1e-05) * own_gain[None, :]).astype(jnp.bfloat16)
    normed = lax.all_gather(normed, "req", axis=0, axis_index_groups=in_plane, tiled=True)
    normed = lax.all_gather(normed, "tp", axis=1, tiled=True)
    projected = jnp.dot(normed, decoder_weight, preferred_element_type=jnp.float32)
    cosine_table, sine_table = rope_tables(seq_slots)
    cosine_table = jnp.tile(cosine_table, (plane, 1))
    sine_table = jnp.tile(sine_table, (plane, 1))
    turned = apply_rope(projected, cosine_table, sine_table).astype(jnp.bfloat16)
    turned = lax.all_to_all(
        turned.reshape(plane, seq_slots, -1),
        "req",
        split_axis=0,
        concat_axis=0,
        axis_index_groups=in_plane,
        tiled=True,
    )
    return jnp.swapaxes(turned, 0, 1).reshape(seq_slots, -1)


MESH = pl.DeviceIdType.MESH
BF16 = jnp.bfloat16
F32 = jnp.float32


def dot(a, b):
    return jnp.dot(a, b, preferred_element_type=F32)


def fused_kernel(
    dims,
    context,
    residual,
    out_weight,
    scale,
    prompt,
    gain,
    qkv_weight,
    target_row,
    image_from,
    slot_from,
    cosine,
    sine,
    out,
    slab,
    out_slab,
    blocks,
    partials,
    returned,
    mean_residual,
    merged,
    outgoing,
    arrived,
    images,
    squares,
    image_squares,
    texts,
    pictures,
    sources,
    total,
    turned,
    slab_in_send,
    slab_in_recv,
    slab_local,
    slab_send,
    slab_recv,
    out_slab_send,
    out_slab_recv,
    out_slab_local,
    block_send,
    block_recv,
    partial_send,
    partial_recv,
    place_send,
    place_recv,
    square_send,
    square_recv,
    text_send,
    text_recv,
    text_cross,
    picture_send,
    picture_recv,
    picture_cross,
    source_send,
    source_recv,
    turned_send,
    turned_recv,
    turned_local,
):
    requests, cores, plane, depth = dims
    req = lax.axis_index("req")
    core = lax.axis_index("tp")
    level = req // plane
    spot = req % plane
    sibling = 1 - core
    rows = blocks.shape[1]
    width = blocks.shape[2]
    depth_rows = qkv_weight.shape[0]
    share = slab.shape[-1]
    columns = out_weight.shape[1]
    seq = out.shape[0]
    half = width // 2
    held = depth // cores
    others = [
        ((spot // 2 + ry) % 2) * 2 + (spot % 2 + rx) % 2 for ry, rx in ((0, 1), (1, 0), (1, 1))
    ]

    def remote(src, dst, send, recv, to_req, to_core):
        return pltpu.make_async_remote_copy(
            src_ref=src,
            dst_ref=dst,
            send_sem=send,
            recv_sem=recv,
            device_id=(to_req, to_core),
            device_id_type=MESH,
        )

    def arrive(dst, recv):
        remote(dst, dst, slab_local, recv, req, sibling).wait_recv()

    barrier = pltpu.get_barrier_semaphore()
    count = requests * cores

    @pl.loop(1, count)
    def _(offset):
        at = (req * cores + core + offset) % count
        pl.semaphore_signal(
            barrier, inc=1, device_id=(at // cores, at % cores), device_id_type=MESH
        )

    pl.semaphore_wait(barrier, count - 1)

    out_sends = []
    for i, other in enumerate(others):
        out_sends.append(
            remote(
                out_weight,
                out_slab.at[spot],
                out_slab_send.at[i],
                out_slab_recv.at[spot],
                level * plane + other,
                core,
            )
        )
        out_sends[-1].start()
    out_own = pltpu.make_async_copy(out_weight, out_slab.at[spot], out_slab_local)
    out_own.start()

    first_patch = 4 * lax.broadcasted_iota(jnp.int32, (rows, 4 * rows), 0)
    patch = lax.broadcasted_iota(jnp.int32, (rows, 4 * rows), 1)
    inside = (patch >= first_patch) & (patch < first_patch + 4)
    averaging = jnp.where(inside, 0.25, 0.0).astype(BF16)
    for i in range(width // 512):
        cols = slice(i * 512, (i + 1) * 512)
        blocks[level, :, cols] = dot(averaging, context[:, cols]).astype(BF16)

    def pass_on(buffer, send, recv, hop, first):
        if hop > 1:

            @pl.when(level - (hop - 1) >= 0)
            def _():
                arrive(buffer.at[level - (hop - 1)], recv.at[level - (hop - 1)])

            @pl.when(level + (hop - 1) < depth)
            def _():
                arrive(buffer.at[level + (hop - 1)], recv.at[level + (hop - 1)])

        if hop == depth:
            return

        @pl.when((level - (hop - 1) >= 0) & (level + 1 < depth))
        def _():
            at = level - (hop - 1)
            remote(
                buffer.at[at], buffer.at[at], send.at[hop - 1, 0], recv.at[at], req + plane, core
            ).start()

        @pl.when((level + (hop - 1) < depth) & (level - 1 >= 0))
        def _():
            at = level + (hop - 1)
            remote(
                buffer.at[at], buffer.at[at], send.at[hop - 1, 1], recv.at[at], req - plane, core
            ).start()

    def passed(buffer, send, recv):
        for hop in range(1, depth):

            @pl.when((level - (hop - 1) >= 0) & (level + 1 < depth))
            def _():
                at = level - (hop - 1)
                remote(
                    buffer.at[at], buffer.at[at], send.at[hop - 1, 0], recv.at[at], req, sibling
                ).wait_send()

            @pl.when((level + (hop - 1) < depth) & (level - 1 >= 0))
            def _():
                at = level + (hop - 1)
                remote(
                    buffer.at[at], buffer.at[at], send.at[hop - 1, 1], recv.at[at], req, sibling
                ).wait_send()

    pass_on(blocks, block_send, block_recv, 1, True)

    slab_sends = []
    for i, other in enumerate(others):
        at = pl.multiple_of(other * share, share)
        slab_sends.append(
            remote(
                qkv_weight.at[:, pl.ds(at, share)],
                slab.at[level, spot],
                slab_in_send.at[i],
                slab_in_recv.at[spot],
                level * plane + other,
                core,
            )
        )
        slab_sends[-1].start()
    slab_own = pltpu.make_async_copy(
        qkv_weight.at[:, pl.ds(pl.multiple_of(spot * share, share), share)],
        slab.at[level, spot],
        slab_local,
    )
    slab_own.start()

    for i in range(width // 512):
        cols = slice(i * 512, (i + 1) * 512)
        mean_residual[:, cols] = dot(averaging, residual[:, cols])

    own_gain = gain[:, pl.ds(pl.multiple_of(core * width, width), width)]

    def squares_of(values):
        return jnp.broadcast_to(
            jnp.sum(values * values, axis=-1, keepdims=True), (values.shape[0], 128)
        )

    def share_squares(buffer, i):
        copy = remote(
            buffer.at[0], buffer.at[1], square_send.at[i], square_recv.at[i], req, sibling
        )
        copy.start()
        copy.wait()
        mean_square = (buffer[0, :, :1] + buffer[1, :, :1]) / (width * cores)
        return lax.rsqrt(mean_square + 1e-05)

    squares[0] = squares_of(prompt[...].astype(F32))
    factor = share_squares(squares, 0)
    for i in range(width // 512):
        cols = slice(i * 512, (i + 1) * 512)
        texts[spot, core, :, cols] = (
            prompt[:, cols].astype(F32) * factor * own_gain[:, cols]
        ).astype(BF16)
    sources[spot] = jnp.broadcast_to(slot_from[...], sources.shape[1:]).astype(BF16)

    for hop in range(2, depth + 1):
        pass_on(blocks, block_send, block_recv, hop, True)
    passed(blocks, block_send, block_recv)

    slab_own.wait()
    for other in others:
        arrive(slab.at[level, other], slab_in_recv.at[other])
    pass_on(slab, slab_send, slab_recv, 1, False)

    out_own.wait()
    for other in others:
        arrive(out_slab.at[other], out_slab_recv.at[other])

    def spread(buffer, send, recv):
        copies = []
        for i, other in enumerate(others):
            own = buffer.at[spot, core]
            copies.append(
                remote(own, own, send.at[i], recv.at[spot, core], level * plane + other, core)
            )
            copies[-1].start()
        return copies

    def cross(buffer, place, send, recv):
        part = buffer.at[place, core]
        copy = remote(part, part, send, recv.at[place, core], req, sibling)
        copy.start()
        return copy

    sends = []
    for i, other in enumerate(others):
        own = sources.at[spot]
        sends.append(
            remote(
                own, own, source_send.at[i], source_recv.at[spot], level * plane + other, core
            )
        )
        sends[-1].start()
    sends.extend(spread(texts, text_send, text_recv))
    sends.append(cross(texts, spot, text_cross.at[0], text_recv))

    owner_core = level // held
    lane = level % held

    @pl.loop(0, depth)
    def _(step):
        target = (level + 1 + step) % depth
        for i in range(plane):
            partials[target, :, i * columns : (i + 1) * columns] = dot(
                blocks[target], out_slab[i]
            ).astype(BF16)
        own = (target == level) & (owner_core == core)

        @pl.when(own)
        def _():
            pltpu.make_async_copy(
                partials.at[target], returned.at[lane, core], partial_recv.at[lane, core]
            ).start()

        @pl.when(jnp.logical_not(own))
        def _():
            remote(
                partials.at[target],
                returned.at[lane, core],
                partial_send.at[target],
                partial_recv.at[lane, core],
                target * plane + spot,
                owner_core,
            ).start()

    for i in range(held):
        for j in range(cores):
            arrive(returned.at[i, j], partial_recv.at[i, j])
    for i in range(held):
        cols = slice(i * half, (i + 1) * half)
        added = returned[i, 0].astype(F32)
        for j in range(1, cores):
            added = added + returned[i, j].astype(F32)
        merged[:, cols] = (mean_residual[:, cols] + scale[:, cols] * added).astype(BF16)

    block_rows = outgoing.shape[1]
    slot = lax.broadcasted_iota(jnp.int32, (requests * block_rows, rows), 0)
    placed = jnp.zeros((requests * block_rows, half), F32)
    for i in range(2):
        place = jnp.where(slot == target_row[...] + i * (block_rows // 2), 1.0, 0.0).astype(BF16)
        placed = placed + dot(place, merged[:, i * half : (i + 1) * half])
    outgoing[...] = placed.astype(BF16).reshape(outgoing.shape)

    @pl.loop(1, requests)
    def _(offset):
        to = (req + offset) % requests
        remote(
            outgoing.at[to], arrived.at[req], place_send.at[to], place_recv.at[req], to, core
        ).start()

    place_own = pltpu.make_async_copy(outgoing.at[req], arrived.at[req], place_send.at[req])
    place_own.start()
    pass_on(slab, slab_send, slab_recv, 2, False)
    place_own.wait()

    @pl.loop(1, requests)
    def _(offset):
        source = (req + offset) % requests
        arrive(arrived.at[source], place_recv.at[source])

    slot = lax.broadcasted_iota(jnp.int32, (images.shape[0], requests * block_rows), 1)
    for i in range(2):
        pick = jnp.where(slot == image_from[...] + i * (block_rows // 2), 1.0, 0.0).astype(BF16)
        images[:, i * half : (i + 1) * half] = dot(
            pick, arrived[...].reshape(requests * block_rows, half)
        )
    image_squares[0] = squares_of(images[...])
    factor = share_squares(image_squares, 1)
    for i in range(2):
        cols = slice(i * half, (i + 1) * half)
        pictures[spot, core, :, cols] = (images[:, cols] * factor * own_gain[:, cols]).astype(BF16)
    sends.extend(spread(pictures, picture_send, picture_recv))
    sends.append(cross(pictures, spot, picture_cross.at[0], picture_recv))

    for i, other in enumerate(others):
        arrive(texts.at[other, core], text_recv.at[other, core])
        sends.append(cross(texts, other, text_cross.at[i + 1], text_recv))
        arrive(sources.at[other], source_recv.at[other])
    for i, other in enumerate(others):
        arrive(pictures.at[other, core], picture_recv.at[other, core])
        sends.append(cross(pictures, other, picture_cross.at[i + 1], picture_recv))
    for hop in range(3, depth):
        pass_on(slab, slab_send, slab_recv, hop, False)
    for place in [spot] + others:
        arrive(texts.at[place, sibling], text_recv.at[place, sibling])
        arrive(pictures.at[place, sibling], picture_recv.at[place, sibling])

    tile = 256
    level_rows = plane * depth_rows
    seq_texts = texts.shape[2]
    lanes = lax.broadcasted_iota(jnp.int32, (seq, 128), 1).astype(F32)

    def multiply(at, place, first):
        part = at // held
        base = pl.multiple_of((at % held) * level_rows, level_rows)
        source = sources[place].astype(F32)
        picks = [
            jnp.where(source == lanes + i * 128, 1.0, 0.0).astype(BF16)
            for i in range(seq_texts // 128)
        ]
        image_pick = jnp.where(source == -1.0 - lanes, 1.0, 0.0).astype(BF16)
        text_pick = jnp.concatenate(picks, axis=1)
        a = dot(text_pick, texts[place, part, :, pl.ds(base, level_rows)]) + dot(
            image_pick, pictures[place, part, :, pl.ds(base, level_rows)]
        )
        a = a.astype(BF16)
        for n in range(share // tile):
            cols = slice(n * tile, (n + 1) * tile)
            b = slab[at, :, :, cols].reshape(level_rows, tile)
            if first:
                total[place, :, cols] = dot(a, b)
            else:
                total[place, :, cols] += dot(a, b)

    def multiply_all(at, first):
        @pl.loop(0, plane)
        def _(place):
            multiply(at, place, first)

    multiply_all(level, True)
    for hop in range(1, depth - 1):

        @pl.when(level - hop >= 0)
        def _():
            multiply_all(level - hop, False)

        @pl.when(level + hop < depth)
        def _():
            multiply_all(level + hop, False)

    pass_on(slab, slab_send, slab_recv, depth, False)
    last = depth - 1 - level
    here = pl.ds(pl.multiple_of(spot * share, share), share)

    @pl.loop(0, plane)
    def _(step):
        place = (spot + 1 + step) % plane

        @pl.when((level == 0) | (level == depth - 1))
        def _():
            multiply(last, place, False)

        for head in range(share // HEAD):
            cols = slice(head * HEAD, (head + 1) * HEAD)
            values = total[place, :, cols]
            if head <= GROUP:
                values = values * cosine[...] + pltpu.roll(values, HEAD // 2, 1) * sine[...]
            turned[place, :, cols] = values.astype(BF16)

        @pl.when(step < plane - 1)
        def _():
            remote(
                turned.at[place],
                out.at[:, here],
                turned_send.at[place],
                turned_recv.at[spot],
                level * plane + place,
                core,
            ).start()

    turned_own = pltpu.make_async_copy(turned.at[spot], out.at[:, here], turned_local)
    turned_own.start()

    for copy in out_sends + slab_sends + sends:
        copy.wait_send()
    passed(slab, slab_send, slab_recv)

    @pl.loop(0, depth)
    def _(target):
        @pl.when(jnp.logical_not((target == level) & (owner_core == core)))
        def _():
            remote(
                partials.at[target],
                returned.at[lane, core],
                partial_send.at[target],
                partial_recv.at[lane, core],
                req,
                sibling,
            ).wait_send()

    @pl.loop(1, requests)
    def _(offset):
        to = (req + offset) % requests
        remote(
            outgoing.at[to], arrived.at[req], place_send.at[to], place_recv.at[req], req, sibling
        ).wait_send()

    for other in others:
        remote(
            turned.at[other],
            out.at[:, here],
            turned_send.at[other],
            turned_recv.at[spot],
            req,
            sibling,
        ).wait_send()
    turned_own.wait()
    for other in others:
        there = pl.ds(pl.multiple_of(other * share, share), share)
        arrive(out.at[:, there], turned_recv.at[other])


def fused_shards(
    vit_context,
    vision_residual,
    out_weight,
    layer_scale,
    prompt,
    prompt_len,
    image_at,
    grid_sizes,
    image_owner,
    norm_gain,
    qkv_weight,
):
    requests = lax.axis_size("req")
    cores = lax.axis_size("tp")
    device_index = lax.axis_index("req")
    tp_index = lax.axis_index("tp")
    patches, width = vit_context.shape
    rows = patches // 4
    share = (GROUP + 2) * HEAD
    plane = qkv_weight.shape[1] // share
    depth = requests // plane
    seq_slots = prompt.shape[1] + IMG_MAX

    counts, starts = request_plan(grid_sizes, image_owner, requests)
    request_ends = starts + counts
    capacity = (IMG_MAX + requests - 1) // requests
    request_ids = jnp.arange(requests, dtype=jnp.int32)
    group_index = jnp.arange(rows, dtype=jnp.int32) * requests + device_index
    destination = jnp.sum((request_ends[None, :] <= group_index[:, None]).astype(jnp.int32), axis=1)
    owned_start = jnp.sum(
        jnp.where(destination[:, None] == request_ids[None, :], starts[None, :], 0), axis=1
    )
    target = destination * 2 * capacity + (group_index - owned_start) // requests
    usable = destination < requests
    target = jnp.where(usable, target, -requests * 2 * capacity)
    own_request = request_ids == device_index
    own_count = jnp.sum(jnp.where(own_request, counts, 0))
    own_start = jnp.sum(jnp.where(own_request, starts, 0))
    image_from = image_at[0]
    prompt_count = prompt_len[0]
    image_row = jnp.arange(IMG_MAX, dtype=jnp.int32)
    from_flat = (own_start + image_row) % requests * 2 * capacity + image_row // requests
    from_flat = jnp.where(image_row < own_count, from_flat, -requests * 2 * capacity)
    slot_index = jnp.arange(seq_slots, dtype=jnp.int32)
    slot_image = slot_index - image_from
    in_image = (slot_image >= 0) & (slot_image < own_count)
    slot_row = jnp.where(slot_index < image_from, slot_index, slot_index - own_count)
    slot_from = jnp.where(slot_index < prompt_count + own_count, slot_row, 512)
    slot_from = jnp.where(in_image, -1 - slot_image, slot_from)
    cosine_table, sine_table = rope_tables(seq_slots)
    cosine = jnp.concatenate([cosine_table, cosine_table], axis=1)
    sine = jnp.concatenate([-sine_table, sine_table], axis=1)

    vmem = pl.BlockSpec(memory_space=pltpu.VMEM)
    anywhere = pl.BlockSpec(memory_space=pl.ANY)
    dma = pltpu.SemaphoreType.DMA
    columns = out_weight.shape[1]
    half = width // 2
    return pl.pallas_call(
        functools.partial(fused_kernel, (requests, cores, plane, depth)),
        out_shape=jax.ShapeDtypeStruct((seq_slots, qkv_weight.shape[1]), BF16),
        in_specs=[vmem, vmem, anywhere, vmem, vmem, vmem, anywhere] + [vmem] * 5,
        out_specs=anywhere,
        scratch_shapes=[
            pltpu.VMEM((depth, plane, qkv_weight.shape[0], share), BF16),
            pltpu.VMEM((plane, width, columns), BF16),
            pltpu.VMEM((depth, rows, width), BF16),
            pltpu.VMEM((depth, rows, plane * columns), BF16),
            pltpu.VMEM((depth // cores, cores, rows, plane * columns), BF16),
            pltpu.VMEM((rows, width), F32),
            pltpu.VMEM((rows, width), BF16),
            pltpu.VMEM((requests, 2 * capacity, half), BF16),
            pltpu.VMEM((requests, 2 * capacity, half), BF16),
            pltpu.VMEM((IMG_MAX, width), F32),
            pltpu.VMEM((2, prompt.shape[1], 128), F32),
            pltpu.VMEM((2, IMG_MAX, 128), F32),
            pltpu.VMEM((plane, cores, prompt.shape[1], width), BF16),
            pltpu.VMEM((plane, cores, IMG_MAX, width), BF16),
            pltpu.VMEM((plane, seq_slots, 128), BF16),
            pltpu.VMEM((plane, seq_slots, share), F32),
            pltpu.VMEM((plane, seq_slots, share), BF16),
            dma((plane,)),
            dma((plane,)),
            dma,
            dma((depth, 2)),
            dma((depth,)),
            dma((plane,)),
            dma((plane,)),
            dma,
            dma((depth, 2)),
            dma((depth,)),
            dma((depth,)),
            dma((depth // cores, cores)),
            dma((requests,)),
            dma((requests,)),
            dma((2,)),
            dma((2,)),
            dma((plane,)),
            dma((plane, cores)),
            dma((plane,)),
            dma((plane,)),
            dma((plane, cores)),
            dma((plane,)),
            dma((plane,)),
            dma((plane,)),
            dma((plane,)),
            dma((plane,)),
            dma,
        ],
        compiler_params=pltpu.CompilerParams(
            collective_id=0, has_side_effects=True, vmem_limit_bytes=58 * 1024 * 1024
        ),
        cost_estimate=pl.CostEstimate(
            flops=30 * 10**9, bytes_accessed=20 * 2**20, transcendentals=0
        ),
    )(
        vit_context,
        vision_residual,
        out_weight,
        layer_scale[None, :],
        prompt[0],
        norm_gain[None, :],
        qkv_weight,
        target[None, :],
        from_flat[:, None],
        slot_from[:, None],
        cosine,
        sine,
    )


def solution(mesh):
    requests, cores = mesh.shape["req"], mesh.shape["tp"]

    def shards(*arrays):
        patches, width = arrays[0].shape
        plane = arrays[-1].shape[1] // ((GROUP + 2) * HEAD)
        fits = (
            cores == 2
            and plane == 4
            and requests // plane % cores == 0
            and arrays[2].shape[1] * requests == width * cores
            and arrays[2].shape[1] % 128 == 0
            and IMG_MAX % requests == 0
            and (IMG_MAX // requests) % 8 == 0
            and IMG_MAX == 128
            and arrays[4].shape[1] in (128, 256)
        )
        return (fused_shards if fits else collective_shards)(*arrays)

    in_specs = (
        P("req", "tp"),
        P("req", "tp"),
        P("tp", "req"),
        P("tp"),
        P("req", None, "tp"),
        P("req"),
        P("req"),
        P(),
        P(),
        P(),
        P("req", "tp"),
    )
    out_specs = P("req", "tp")
    return jax.shard_map(shards, mesh=mesh, in_specs=in_specs, out_specs=out_specs, check_vma=False)
```

```python
import functools

import jax
import jax.numpy as jnp
from jax import lax
from jax.experimental import pallas as pl
from jax.experimental.pallas import tpu as pltpu
from jax.sharding import PartitionSpec as P

HEAD = 128
GROUP = 4
IMG_MAX = 128


def request_plan(grid_sizes, image_owner, requests):
    image_rows = grid_sizes[:, 0] * grid_sizes[:, 1]
    member = (image_owner[:, None] == jnp.arange(requests, dtype=jnp.int32)[None, :]).astype(
        jnp.int32
    )
    counts = jnp.sum(image_rows[:, None] * member, axis=0)
    starts = jnp.cumsum(counts) - counts
    return (counts, starts)


def rope_tables(count):
    half_size = HEAD // 2
    exponent = jnp.arange(half_size, dtype=jnp.float32) * (2.0 / HEAD)
    frequency = jnp.exp(-exponent * jnp.log(jnp.float32(500000.0)))
    angles = jnp.arange(count, dtype=jnp.float32)[:, None] * frequency[None, :]
    return (jnp.cos(angles), jnp.sin(angles))


def apply_rope(projected, cosine_table, sine_table):
    seq_rows = projected.shape[0]
    head_blocks = projected.reshape(seq_rows, -1, GROUP + 2, HEAD)
    turning = head_blocks[:, :, : GROUP + 1, :]
    first_half = turning[..., : HEAD // 2]
    second_half = turning[..., HEAD // 2 :]
    cosine_wide = cosine_table[:, None, None, :]
    sine_wide = sine_table[:, None, None, :]
    turned = jnp.concatenate(
        [
            first_half * cosine_wide - second_half * sine_wide,
            second_half * cosine_wide + first_half * sine_wide,
        ],
        axis=-1,
    )
    head_blocks = jnp.concatenate([turned, head_blocks[:, :, GROUP + 1 :, :]], axis=2)
    return head_blocks.reshape(seq_rows, -1)


def collective_shards(
    vit_context,
    vision_residual,
    out_weight,
    layer_scale,
    prompt,
    prompt_len,
    image_at,
    grid_sizes,
    image_owner,
    norm_gain,
    qkv_weight,
):
    requests = lax.axis_size("req")
    device_index = lax.axis_index("req")
    tp_index = lax.axis_index("tp")
    feature_width = vit_context.shape[1]
    plane = qkv_weight.shape[1] // ((GROUP + 2) * HEAD)
    depth = requests // plane
    in_plane = [[d * plane + i for i in range(plane)] for d in range(depth)]
    in_depth = [[d * plane + i for d in range(depth)] for i in range(plane)]
    weight_rows = qkv_weight.shape[0]
    weight_parts = jnp.swapaxes(qkv_weight.reshape(weight_rows, plane, -1), 0, 1)
    weight_parts = lax.all_to_all(
        weight_parts, "req", split_axis=0, concat_axis=0, axis_index_groups=in_plane, tiled=True
    )
    decoder_weight = lax.all_gather(
        weight_parts.reshape(plane * weight_rows, -1),
        "req",
        axis=0,
        axis_index_groups=in_depth,
        tiled=True,
    )
    merged_context = jnp.mean(
        vit_context.astype(jnp.float32).reshape(-1, 4, feature_width), axis=1
    ).astype(jnp.bfloat16)
    merged_residual = jnp.mean(
        vision_residual.astype(jnp.float32).reshape(-1, 4, feature_width), axis=1
    )
    partial_value = jnp.dot(
        lax.all_gather(merged_context, "req", axis=0, axis_index_groups=in_depth, tiled=True),
        lax.all_gather(out_weight, "req", axis=1, axis_index_groups=in_plane, tiled=True),
        preferred_element_type=jnp.float32,
    )
    returned = lax.all_to_all(
        partial_value.astype(jnp.bfloat16).reshape(depth, merged_context.shape[0], -1),
        "req",
        split_axis=0,
        concat_axis=0,
        axis_index_groups=in_depth,
        tiled=True,
    )
    returned = jnp.swapaxes(returned, 0, 1).reshape(merged_context.shape[0], -1)
    summed = lax.psum(returned, "tp").astype(jnp.float32)
    own_share = lax.dynamic_slice_in_dim(summed, tp_index * feature_width, feature_width, 1)
    merged = (merged_residual + layer_scale[None, :] * own_share).astype(jnp.bfloat16)
    merged_count = merged.shape[0]
    counts, starts = request_plan(grid_sizes, image_owner, requests)
    request_ends = starts + counts
    capacity = (IMG_MAX + requests - 1) // requests
    request_ids = jnp.arange(requests, dtype=jnp.int32)
    group_index = jnp.arange(merged_count, dtype=jnp.int32) * requests + device_index
    destination = jnp.sum((request_ends[None, :] <= group_index[:, None]).astype(jnp.int32), axis=1)
    owned_start = jnp.sum(
        jnp.where(destination[:, None] == request_ids[None, :], starts[None, :], 0), axis=1
    )
    target = destination * capacity + (group_index - owned_start) // requests
    usable = destination < requests
    send_slots = jnp.arange(requests * capacity, dtype=jnp.int32)
    placing = ((send_slots[:, None] == target[None, :]) & usable[None, :]).astype(jnp.bfloat16)
    outgoing = jnp.dot(placing, merged, preferred_element_type=jnp.float32).astype(jnp.bfloat16)
    arrived = lax.all_to_all(
        outgoing.reshape(requests, capacity, feature_width),
        "req",
        split_axis=0,
        concat_axis=0,
        tiled=True,
    )
    arrived = arrived.reshape(requests * capacity, feature_width)
    own_request = request_ids == device_index
    own_count = jnp.sum(jnp.where(own_request, counts, 0))
    own_start = jnp.sum(jnp.where(own_request, starts, 0))
    image_from = image_at[0]
    prompt_count = prompt_len[0]
    seq_slots = prompt.shape[1] + IMG_MAX
    slot_index = jnp.arange(seq_slots, dtype=jnp.int32)
    image_row = slot_index - image_from
    in_image = (image_row >= 0) & (image_row < own_count)
    is_live = slot_index < prompt_count + own_count
    from_prompt = is_live & jnp.logical_not(in_image)
    flat_index = (own_start + image_row) % requests * capacity + image_row // requests
    image_pick = ((flat_index[:, None] == send_slots[None, :]) & in_image[:, None]).astype(
        jnp.bfloat16
    )
    prompt_row = jnp.where(slot_index < image_from, slot_index, slot_index - own_count)
    prompt_ids = jnp.arange(prompt.shape[1], dtype=jnp.int32)
    prompt_pick = ((prompt_row[:, None] == prompt_ids[None, :]) & from_prompt[:, None]).astype(
        jnp.bfloat16
    )
    embedded = (
        jnp.dot(image_pick, arrived, preferred_element_type=jnp.float32)
        + jnp.dot(prompt_pick, prompt[0], preferred_element_type=jnp.float32)
    ).astype(jnp.bfloat16)
    values = embedded.astype(jnp.float32)
    square_sum = lax.psum(jnp.sum(values * values, axis=-1, keepdims=True), "tp")
    mean_square = square_sum / (feature_width * lax.axis_size("tp"))
    own_gain = lax.dynamic_slice_in_dim(norm_gain, tp_index * feature_width, feature_width, 0)
    normed = (values * lax.rsqrt(mean_square + 1e-05) * own_gain[None, :]).astype(jnp.bfloat16)
    normed = lax.all_gather(normed, "req", axis=0, axis_index_groups=in_plane, tiled=True)
    normed = lax.all_gather(normed, "tp", axis=1, tiled=True)
    projected = jnp.dot(normed, decoder_weight, preferred_element_type=jnp.float32)
    cosine_table, sine_table = rope_tables(seq_slots)
    cosine_table = jnp.tile(cosine_table, (plane, 1))
    sine_table = jnp.tile(sine_table, (plane, 1))
    turned = apply_rope(projected, cosine_table, sine_table).astype(jnp.bfloat16)
    turned = lax.all_to_all(
        turned.reshape(plane, seq_slots, -1),
        "req",
        split_axis=0,
        concat_axis=0,
        axis_index_groups=in_plane,
        tiled=True,
    )
    return jnp.swapaxes(turned, 0, 1).reshape(seq_slots, -1)


MESH = pl.DeviceIdType.MESH
BF16 = jnp.bfloat16
F32 = jnp.float32


def dot(a, b):
    return jnp.dot(a, b, preferred_element_type=F32)


def fused_kernel(
    dims,
    context,
    residual,
    out_weight,
    scale,
    prompt,
    gain,
    qkv_weight,
    target_row,
    image_from,
    slot_from,
    cosine,
    sine,
    out,
    slab,
    out_slab,
    blocks,
    partials,
    returned,
    mean_residual,
    merged,
    outgoing,
    arrived,
    images,
    squares,
    image_squares,
    texts,
    pictures,
    sources,
    total,
    turned,
    assembled,
    slab_in_send,
    slab_in_recv,
    slab_local,
    slab_send,
    slab_recv,
    out_slab_send,
    out_slab_recv,
    out_slab_local,
    block_send,
    block_recv,
    partial_send,
    partial_recv,
    place_send,
    place_recv,
    square_send,
    square_recv,
    text_send,
    text_recv,
    text_cross,
    picture_send,
    picture_recv,
    picture_cross,
    source_send,
    source_recv,
    turned_send,
    turned_recv,
    turned_local,
    slab_far_send,
    slab_far_recv,
    block_far_send,
    block_far_recv,
):
    requests, cores, plane, depth = dims
    req = lax.axis_index("req")
    core = lax.axis_index("tp")
    level = req // plane
    spot = req % plane
    sibling = 1 - core
    rows = blocks.shape[1]
    width = blocks.shape[2]
    depth_rows = qkv_weight.shape[0]
    share = slab.shape[-1]
    columns = out_weight.shape[1]
    seq = out.shape[0]
    half = width // 2
    held = depth // cores
    others = [
        ((spot // 2 + ry) % 2) * 2 + (spot % 2 + rx) % 2 for ry, rx in ((0, 1), (1, 0), (1, 1))
    ]

    def remote(src, dst, send, recv, to_req, to_core):
        return pltpu.make_async_remote_copy(
            src_ref=src,
            dst_ref=dst,
            send_sem=send,
            recv_sem=recv,
            device_id=(to_req, to_core),
            device_id_type=MESH,
        )

    def arrive(dst, recv):
        remote(dst, dst, slab_local, recv, req, sibling).wait_recv()

    barrier = pltpu.get_barrier_semaphore()
    count = requests * cores

    @pl.loop(1, count)
    def _(offset):
        at = (req * cores + core + offset) % count
        pl.semaphore_signal(
            barrier, inc=1, device_id=(at // cores, at % cores), device_id_type=MESH
        )

    pl.semaphore_wait(barrier, count - 1)

    slab_sends = []
    for i, other in enumerate(others):
        at = pl.multiple_of(other * share, share)
        slab_sends.append(
            remote(
                qkv_weight.at[:, pl.ds(at, share)],
                slab.at[level, spot],
                slab_in_send.at[i],
                slab_in_recv.at[spot],
                level * plane + other,
                core,
            )
        )
        slab_sends[-1].start()
    slab_own = pltpu.make_async_copy(
        qkv_weight.at[:, pl.ds(pl.multiple_of(spot * share, share), share)],
        slab.at[level, spot],
        slab_local,
    )
    slab_own.start()

    out_sends = []
    for i, other in enumerate(others):
        out_sends.append(
            remote(
                out_weight,
                out_slab.at[spot],
                out_slab_send.at[i],
                out_slab_recv.at[spot],
                level * plane + other,
                core,
            )
        )
        out_sends[-1].start()
    out_own = pltpu.make_async_copy(out_weight, out_slab.at[spot], out_slab_local)
    out_own.start()

    first_patch = 4 * lax.broadcasted_iota(jnp.int32, (rows, 4 * rows), 0)
    patch = lax.broadcasted_iota(jnp.int32, (rows, 4 * rows), 1)
    inside = (patch >= first_patch) & (patch < first_patch + 4)
    averaging = jnp.where(inside, 0.25, 0.0).astype(BF16)
    for i in range(width // 512):
        cols = slice(i * 512, (i + 1) * 512)
        blocks[level, :, cols] = dot(averaging, context[:, cols]).astype(BF16)

    def hand(part, send, recv, to_level):
        return remote(part, part, send, recv, to_level * plane + spot, core)

    def near_copies(buffer, send, recv):
        own = buffer.at[level]
        for d in (1, 2):
            yield level + d < depth, hand(own, send.at[d - 1, 0], recv.at[level], level + d)
            yield level - d >= 0, hand(own, send.at[d - 1, 1], recv.at[level], level - d)

    def near_start(buffer, send, recv):
        for there, copy in near_copies(buffer, send, recv):
            pl.when(there)(copy.start)

    def near_sent(buffer, send, recv):
        for there, copy in near_copies(buffer, send, recv):
            pl.when(there)(copy.wait_send)

    def far_copies(buffer, send, far_recv):
        pieces = far_recv.shape[0]
        size = buffer.shape[-1] // pieces
        for here, at, to in ((2, 0, 3), (1, 3, 0)):
            for i in range(pieces):
                part = buffer.at[at, ..., pl.ds(i * size, size)]
                yield level == here, hand(part, send.at[i], far_recv.at[i], to)

    def far_start(buffer, recv, send, far_recv):
        @pl.when(level == 2)
        def _():
            arrive(buffer.at[0], recv.at[0])

        @pl.when(level == 1)
        def _():
            arrive(buffer.at[3], recv.at[3])

        for there, copy in far_copies(buffer, send, far_recv):
            pl.when(there)(copy.start)

    def far_sent(buffer, send, far_recv):
        for there, copy in far_copies(buffer, send, far_recv):
            pl.when(there)(copy.wait_send)

    def near_arrive(buffer, recv, d):
        @pl.when((level - d >= 0) & ((d == 1) | (level == 3)))
        def _():
            arrive(buffer.at[level - d], recv.at[level - d])

        @pl.when((level + d < depth) & ((d == 1) | (level == 0)))
        def _():
            arrive(buffer.at[level + d], recv.at[level + d])

    def far_arrive(buffer, far_recv, i):
        size = buffer.shape[-1] // far_recv.shape[0]
        for here, at in ((0, 3), (3, 0)):

            @pl.when(level == here)
            def _():
                arrive(buffer.at[at, ..., pl.ds(i * size, size)], far_recv.at[i])

    near_start(blocks, block_send, block_recv)

    for i in range(width // 512):
        cols = slice(i * 512, (i + 1) * 512)
        mean_residual[:, cols] = dot(averaging, residual[:, cols])

    own_gain = gain[:, pl.ds(pl.multiple_of(core * width, width), width)]

    def squares_of(values):
        return jnp.broadcast_to(
            jnp.sum(values * values, axis=-1, keepdims=True), (values.shape[0], 128)
        )

    def share_squares(buffer, i):
        copy = remote(
            buffer.at[0], buffer.at[1], square_send.at[i], square_recv.at[i], req, sibling
        )
        copy.start()
        copy.wait()
        mean_square = (buffer[0, :, :1] + buffer[1, :, :1]) / (width * cores)
        return lax.rsqrt(mean_square + 1e-05)

    squares[0] = squares_of(prompt[...].astype(F32))
    factor = share_squares(squares, 0)
    for i in range(width // 512):
        cols = slice(i * 512, (i + 1) * 512)
        texts[spot, core, :, cols] = (
            prompt[:, cols].astype(F32) * factor * own_gain[:, cols]
        ).astype(BF16)
    sources[spot] = jnp.broadcast_to(slot_from[...], sources.shape[1:]).astype(BF16)

    far_start(blocks, block_recv, block_far_send, block_far_recv)
    near_arrive(blocks, block_recv, 1)
    near_arrive(blocks, block_recv, 2)
    far_arrive(blocks, block_far_recv, 0)

    slab_own.wait()
    for other in others:
        arrive(slab.at[level, other], slab_in_recv.at[other])
    near_start(slab, slab_send, slab_recv)

    out_own.wait()
    for other in others:
        arrive(out_slab.at[other], out_slab_recv.at[other])

    def spread(buffer, send, recv):
        copies = []
        for i, other in enumerate(others):
            own = buffer.at[spot, core]
            copies.append(
                remote(own, own, send.at[i], recv.at[spot, core], level * plane + other, core)
            )
            copies[-1].start()
        return copies

    def cross(buffer, place, send, recv):
        part = buffer.at[place, core]
        copy = remote(part, part, send, recv.at[place, core], req, sibling)
        copy.start()
        return copy

    sends = []
    for i, other in enumerate(others):
        own = sources.at[spot]
        sends.append(
            remote(
                own, own, source_send.at[i], source_recv.at[spot], level * plane + other, core
            )
        )
        sends[-1].start()
    sends.extend(spread(texts, text_send, text_recv))
    sends.append(cross(texts, spot, text_cross.at[0], text_recv))

    owner_core = level // held
    lane = level % held

    @pl.loop(0, depth)
    def _(step):
        target = (level + 1 + step) % depth
        for i in range(plane):
            partials[target, :, i * columns : (i + 1) * columns] = dot(
                blocks[target], out_slab[i]
            ).astype(BF16)
        own = (target == level) & (owner_core == core)

        @pl.when(own)
        def _():
            pltpu.make_async_copy(
                partials.at[target], returned.at[lane, core], partial_recv.at[lane, core]
            ).start()

        @pl.when(jnp.logical_not(own))
        def _():
            remote(
                partials.at[target],
                returned.at[lane, core],
                partial_send.at[target],
                partial_recv.at[lane, core],
                target * plane + spot,
                owner_core,
            ).start()

    for i in range(held):
        for j in range(cores):
            arrive(returned.at[i, j], partial_recv.at[i, j])
    for i in range(held):
        cols = slice(i * half, (i + 1) * half)
        added = returned[i, 0].astype(F32)
        for j in range(1, cores):
            added = added + returned[i, j].astype(F32)
        merged[:, cols] = (mean_residual[:, cols] + scale[:, cols] * added).astype(BF16)

    block_rows = outgoing.shape[1]
    slot = lax.broadcasted_iota(jnp.int32, (requests * block_rows, rows), 0)
    placed = jnp.zeros((requests * block_rows, half), F32)
    for i in range(2):
        place = jnp.where(slot == target_row[...] + i * (block_rows // 2), 1.0, 0.0).astype(BF16)
        placed = placed + dot(place, merged[:, i * half : (i + 1) * half])
    outgoing[...] = placed.astype(BF16).reshape(outgoing.shape)

    @pl.loop(1, requests)
    def _(offset):
        to = (req + offset) % requests
        remote(
            outgoing.at[to], arrived.at[req], place_send.at[to], place_recv.at[req], to, core
        ).start()

    place_own = pltpu.make_async_copy(outgoing.at[req], arrived.at[req], place_send.at[req])
    place_own.start()
    place_own.wait()

    @pl.loop(1, requests)
    def _(offset):
        source = (req + offset) % requests
        arrive(arrived.at[source], place_recv.at[source])

    slot = lax.broadcasted_iota(jnp.int32, (images.shape[0], requests * block_rows), 1)
    for i in range(2):
        pick = jnp.where(slot == image_from[...] + i * (block_rows // 2), 1.0, 0.0).astype(BF16)
        images[:, i * half : (i + 1) * half] = dot(
            pick, arrived[...].reshape(requests * block_rows, half)
        )
    image_squares[0] = squares_of(images[...])
    factor = share_squares(image_squares, 1)
    for i in range(2):
        cols = slice(i * half, (i + 1) * half)
        pictures[spot, core, :, cols] = (images[:, cols] * factor * own_gain[:, cols]).astype(BF16)
    sends.extend(spread(pictures, picture_send, picture_recv))
    sends.append(cross(pictures, spot, picture_cross.at[0], picture_recv))
    far_start(slab, slab_recv, slab_far_send, slab_far_recv)

    for i, other in enumerate(others):
        arrive(texts.at[other, core], text_recv.at[other, core])
        sends.append(cross(texts, other, text_cross.at[i + 1], text_recv))
        arrive(sources.at[other], source_recv.at[other])
    for i, other in enumerate(others):
        arrive(pictures.at[other, core], picture_recv.at[other, core])
        sends.append(cross(pictures, other, picture_cross.at[i + 1], picture_recv))
    for place in [spot] + others:
        arrive(texts.at[place, sibling], text_recv.at[place, sibling])
        arrive(pictures.at[place, sibling], picture_recv.at[place, sibling])

    tile = 256
    level_rows = plane * depth_rows
    seq_texts = texts.shape[2]
    lanes = lax.broadcasted_iota(jnp.int32, (seq, 128), 1).astype(F32)

    def level_of(at, place):
        part = at // held
        base = pl.multiple_of((at % held) * level_rows, level_rows)
        source = sources[place].astype(F32)
        picks = [
            jnp.where(source == lanes + i * 128, 1.0, 0.0).astype(BF16)
            for i in range(seq_texts // 128)
        ]
        image_pick = jnp.where(source == -1.0 - lanes, 1.0, 0.0).astype(BF16)
        text_pick = jnp.concatenate(picks, axis=1)
        a = dot(text_pick, texts[place, part, :, pl.ds(base, level_rows)]) + dot(
            image_pick, pictures[place, part, :, pl.ds(base, level_rows)]
        )
        return a.astype(BF16)

    def multiply_all(at, first):
        @pl.loop(0, plane)
        def _(place):
            a = level_of(at, place)
            for n in range(share // tile):
                cols = slice(n * tile, (n + 1) * tile)
                b = slab[at, :, :, cols].reshape(level_rows, tile)
                if first:
                    total[place, :, cols] = dot(a, b)
                else:
                    total[place, :, cols] += dot(a, b)

    multiply_all(level, True)
    for d in (1, 2):
        near_arrive(slab, slab_recv, d)

        @pl.when(level - d >= 0)
        def _():
            multiply_all(level - d, False)

        @pl.when(level + d < depth)
        def _():
            multiply_all(level + d, False)

    at_edge = (level == 0) | (level == depth - 1)
    last = depth - 1 - level

    @pl.when(at_edge)
    def _():
        @pl.loop(0, plane)
        def _(place):
            assembled[place] = level_of(last, place)

    def leave(place, n):
        start = pl.multiple_of(spot * share + n * tile, tile)
        return remote(
            turned.at[place, :, pl.ds(n * tile, tile)],
            out.at[:, pl.ds(start, tile)],
            turned_send.at[place, n],
            turned_recv.at[spot, n],
            level * plane + place,
            core,
        )

    for n in range(share // tile):
        far_arrive(slab, slab_far_recv, n)

        @pl.loop(0, plane)
        def _(step):
            place = (spot + 1 + step) % plane

            @pl.when(at_edge)
            def _():
                cols = slice(n * tile, (n + 1) * tile)
                b = slab[last, :, :, cols].reshape(level_rows, tile)
                total[place, :, cols] += dot(assembled[place], b)

            for head in range(n * tile // HEAD, (n + 1) * tile // HEAD):
                cols = slice(head * HEAD, (head + 1) * HEAD)
                values = total[place, :, cols]
                if head <= GROUP:
                    values = values * cosine[...] + pltpu.roll(values, HEAD // 2, 1) * sine[...]
                turned[place, :, cols] = values.astype(BF16)

            @pl.when(step < plane - 1)
            def _():
                leave(place, n).start()

    here = pl.ds(pl.multiple_of(spot * share, share), share)
    turned_own = pltpu.make_async_copy(turned.at[spot], out.at[:, here], turned_local)
    turned_own.start()

    for copy in out_sends + slab_sends + sends:
        copy.wait_send()
    near_sent(blocks, block_send, block_recv)
    far_sent(blocks, block_far_send, block_far_recv)
    near_sent(slab, slab_send, slab_recv)
    far_sent(slab, slab_far_send, slab_far_recv)

    @pl.loop(0, depth)
    def _(target):
        @pl.when(jnp.logical_not((target == level) & (owner_core == core)))
        def _():
            remote(
                partials.at[target],
                returned.at[lane, core],
                partial_send.at[target],
                partial_recv.at[lane, core],
                req,
                sibling,
            ).wait_send()

    @pl.loop(1, requests)
    def _(offset):
        to = (req + offset) % requests
        remote(
            outgoing.at[to], arrived.at[req], place_send.at[to], place_recv.at[req], req, sibling
        ).wait_send()

    for other in others:
        for n in range(share // tile):
            leave(other, n).wait_send()
    turned_own.wait()
    for other in others:
        for n in range(share // tile):
            start = pl.multiple_of(other * share + n * tile, tile)
            arrive(out.at[:, pl.ds(start, tile)], turned_recv.at[other, n])


def fused_shards(
    vit_context,
    vision_residual,
    out_weight,
    layer_scale,
    prompt,
    prompt_len,
    image_at,
    grid_sizes,
    image_owner,
    norm_gain,
    qkv_weight,
):
    requests = lax.axis_size("req")
    cores = lax.axis_size("tp")
    device_index = lax.axis_index("req")
    tp_index = lax.axis_index("tp")
    patches, width = vit_context.shape
    rows = patches // 4
    share = (GROUP + 2) * HEAD
    plane = qkv_weight.shape[1] // share
    depth = requests // plane
    seq_slots = prompt.shape[1] + IMG_MAX

    counts, starts = request_plan(grid_sizes, image_owner, requests)
    request_ends = starts + counts
    capacity = (IMG_MAX + requests - 1) // requests
    request_ids = jnp.arange(requests, dtype=jnp.int32)
    group_index = jnp.arange(rows, dtype=jnp.int32) * requests + device_index
    destination = jnp.sum((request_ends[None, :] <= group_index[:, None]).astype(jnp.int32), axis=1)
    owned_start = jnp.sum(
        jnp.where(destination[:, None] == request_ids[None, :], starts[None, :], 0), axis=1
    )
    target = destination * 2 * capacity + (group_index - owned_start) // requests
    usable = destination < requests
    target = jnp.where(usable, target, -requests * 2 * capacity)
    own_request = request_ids == device_index
    own_count = jnp.sum(jnp.where(own_request, counts, 0))
    own_start = jnp.sum(jnp.where(own_request, starts, 0))
    image_from = image_at[0]
    prompt_count = prompt_len[0]
    image_row = jnp.arange(IMG_MAX, dtype=jnp.int32)
    from_flat = (own_start + image_row) % requests * 2 * capacity + image_row // requests
    from_flat = jnp.where(image_row < own_count, from_flat, -requests * 2 * capacity)
    slot_index = jnp.arange(seq_slots, dtype=jnp.int32)
    slot_image = slot_index - image_from
    in_image = (slot_image >= 0) & (slot_image < own_count)
    slot_row = jnp.where(slot_index < image_from, slot_index, slot_index - own_count)
    slot_from = jnp.where(slot_index < prompt_count + own_count, slot_row, 512)
    slot_from = jnp.where(in_image, -1 - slot_image, slot_from)
    cosine_table, sine_table = rope_tables(seq_slots)
    cosine = jnp.concatenate([cosine_table, cosine_table], axis=1)
    sine = jnp.concatenate([-sine_table, sine_table], axis=1)

    vmem = pl.BlockSpec(memory_space=pltpu.VMEM)
    anywhere = pl.BlockSpec(memory_space=pl.ANY)
    dma = pltpu.SemaphoreType.DMA
    columns = out_weight.shape[1]
    half = width // 2
    return pl.pallas_call(
        functools.partial(fused_kernel, (requests, cores, plane, depth)),
        out_shape=jax.ShapeDtypeStruct((seq_slots, qkv_weight.shape[1]), BF16),
        in_specs=[vmem, vmem, anywhere, vmem, vmem, vmem, anywhere] + [vmem] * 5,
        out_specs=anywhere,
        scratch_shapes=[
            pltpu.VMEM((depth, plane, qkv_weight.shape[0], share), BF16),
            pltpu.VMEM((plane, width, columns), BF16),
            pltpu.VMEM((depth, rows, width), BF16),
            pltpu.VMEM((depth, rows, plane * columns), BF16),
            pltpu.VMEM((depth // cores, cores, rows, plane * columns), BF16),
            pltpu.VMEM((rows, width), F32),
            pltpu.VMEM((rows, width), BF16),
            pltpu.VMEM((requests, 2 * capacity, half), BF16),
            pltpu.VMEM((requests, 2 * capacity, half), BF16),
            pltpu.VMEM((IMG_MAX, width), F32),
            pltpu.VMEM((2, prompt.shape[1], 128), F32),
            pltpu.VMEM((2, IMG_MAX, 128), F32),
            pltpu.VMEM((plane, cores, prompt.shape[1], width), BF16),
            pltpu.VMEM((plane, cores, IMG_MAX, width), BF16),
            pltpu.VMEM((plane, seq_slots, 128), BF16),
            pltpu.VMEM((plane, seq_slots, share), F32),
            pltpu.VMEM((plane, seq_slots, share), BF16),
            pltpu.VMEM((plane, seq_slots, plane * qkv_weight.shape[0]), BF16),
            dma((plane,)),
            dma((plane,)),
            dma,
            dma((depth, 2)),
            dma((depth,)),
            dma((plane,)),
            dma((plane,)),
            dma,
            dma((depth, 2)),
            dma((depth,)),
            dma((depth,)),
            dma((depth // cores, cores)),
            dma((requests,)),
            dma((requests,)),
            dma((2,)),
            dma((2,)),
            dma((plane,)),
            dma((plane, cores)),
            dma((plane,)),
            dma((plane,)),
            dma((plane, cores)),
            dma((plane,)),
            dma((plane,)),
            dma((plane,)),
            dma((plane, 3)),
            dma((plane, 3)),
            dma,
            dma((3,)),
            dma((3,)),
            dma((1,)),
            dma((1,)),
        ],
        compiler_params=pltpu.CompilerParams(
            collective_id=0, has_side_effects=True, vmem_limit_bytes=58 * 1024 * 1024
        ),
        cost_estimate=pl.CostEstimate(
            flops=30 * 10**9, bytes_accessed=20 * 2**20, transcendentals=0
        ),
    )(
        vit_context,
        vision_residual,
        out_weight,
        layer_scale[None, :],
        prompt[0],
        norm_gain[None, :],
        qkv_weight,
        target[None, :],
        from_flat[:, None],
        slot_from[:, None],
        cosine,
        sine,
    )


def solution(mesh):
    requests, cores = mesh.shape["req"], mesh.shape["tp"]

    def shards(*arrays):
        patches, width = arrays[0].shape
        plane = arrays[-1].shape[1] // ((GROUP + 2) * HEAD)
        fits = (
            cores == 2
            and plane == 4
            and requests // plane == 4
            and arrays[2].shape[1] * requests == width * cores
            and arrays[2].shape[1] % 128 == 0
            and IMG_MAX % requests == 0
            and (IMG_MAX // requests) % 8 == 0
            and IMG_MAX == 128
            and arrays[4].shape[1] in (128, 256)
        )
        return (fused_shards if fits else collective_shards)(*arrays)

    in_specs = (
        P("req", "tp"),
        P("req", "tp"),
        P("tp", "req"),
        P("tp"),
        P("req", None, "tp"),
        P("req"),
        P("req"),
        P(),
        P(),
        P(),
        P("req", "tp"),
    )
    out_specs = P("req", "tp")
    return jax.shard_map(shards, mesh=mesh, in_specs=in_specs, out_specs=out_specs, check_vma=False)
```

```python
import functools

import jax
import jax.numpy as jnp
from jax import lax
from jax.experimental import pallas as pl
from jax.experimental.pallas import tpu as pltpu
from jax.sharding import PartitionSpec as P

HEAD = 128
GROUP = 4
IMG_MAX = 128


def request_plan(grid_sizes, image_owner, requests):
    image_rows = grid_sizes[:, 0] * grid_sizes[:, 1]
    member = (image_owner[:, None] == jnp.arange(requests, dtype=jnp.int32)[None, :]).astype(
        jnp.int32
    )
    counts = jnp.sum(image_rows[:, None] * member, axis=0)
    starts = jnp.cumsum(counts) - counts
    return (counts, starts)


def rope_tables(count):
    half_size = HEAD // 2
    exponent = jnp.arange(half_size, dtype=jnp.float32) * (2.0 / HEAD)
    frequency = jnp.exp(-exponent * jnp.log(jnp.float32(500000.0)))
    angles = jnp.arange(count, dtype=jnp.float32)[:, None] * frequency[None, :]
    return (jnp.cos(angles), jnp.sin(angles))


def apply_rope(projected, cosine_table, sine_table):
    seq_rows = projected.shape[0]
    head_blocks = projected.reshape(seq_rows, -1, GROUP + 2, HEAD)
    turning = head_blocks[:, :, : GROUP + 1, :]
    first_half = turning[..., : HEAD // 2]
    second_half = turning[..., HEAD // 2 :]
    cosine_wide = cosine_table[:, None, None, :]
    sine_wide = sine_table[:, None, None, :]
    turned = jnp.concatenate(
        [
            first_half * cosine_wide - second_half * sine_wide,
            second_half * cosine_wide + first_half * sine_wide,
        ],
        axis=-1,
    )
    head_blocks = jnp.concatenate([turned, head_blocks[:, :, GROUP + 1 :, :]], axis=2)
    return head_blocks.reshape(seq_rows, -1)


def collective_shards(
    vit_context,
    vision_residual,
    out_weight,
    layer_scale,
    prompt,
    prompt_len,
    image_at,
    grid_sizes,
    image_owner,
    norm_gain,
    qkv_weight,
):
    requests = lax.axis_size("req")
    device_index = lax.axis_index("req")
    tp_index = lax.axis_index("tp")
    feature_width = vit_context.shape[1]
    plane = qkv_weight.shape[1] // ((GROUP + 2) * HEAD)
    depth = requests // plane
    in_plane = [[d * plane + i for i in range(plane)] for d in range(depth)]
    in_depth = [[d * plane + i for d in range(depth)] for i in range(plane)]
    weight_rows = qkv_weight.shape[0]
    weight_parts = jnp.swapaxes(qkv_weight.reshape(weight_rows, plane, -1), 0, 1)
    weight_parts = lax.all_to_all(
        weight_parts, "req", split_axis=0, concat_axis=0, axis_index_groups=in_plane, tiled=True
    )
    decoder_weight = lax.all_gather(
        weight_parts.reshape(plane * weight_rows, -1),
        "req",
        axis=0,
        axis_index_groups=in_depth,
        tiled=True,
    )
    merged_context = jnp.mean(
        vit_context.astype(jnp.float32).reshape(-1, 4, feature_width), axis=1
    ).astype(jnp.bfloat16)
    merged_residual = jnp.mean(
        vision_residual.astype(jnp.float32).reshape(-1, 4, feature_width), axis=1
    )
    partial_value = jnp.dot(
        lax.all_gather(merged_context, "req", axis=0, axis_index_groups=in_depth, tiled=True),
        lax.all_gather(out_weight, "req", axis=1, axis_index_groups=in_plane, tiled=True),
        preferred_element_type=jnp.float32,
    )
    returned = lax.all_to_all(
        partial_value.astype(jnp.bfloat16).reshape(depth, merged_context.shape[0], -1),
        "req",
        split_axis=0,
        concat_axis=0,
        axis_index_groups=in_depth,
        tiled=True,
    )
    returned = jnp.swapaxes(returned, 0, 1).reshape(merged_context.shape[0], -1)
    summed = lax.psum(returned, "tp").astype(jnp.float32)
    own_share = lax.dynamic_slice_in_dim(summed, tp_index * feature_width, feature_width, 1)
    merged = (merged_residual + layer_scale[None, :] * own_share).astype(jnp.bfloat16)
    merged_count = merged.shape[0]
    counts, starts = request_plan(grid_sizes, image_owner, requests)
    request_ends = starts + counts
    capacity = (IMG_MAX + requests - 1) // requests
    request_ids = jnp.arange(requests, dtype=jnp.int32)
    group_index = jnp.arange(merged_count, dtype=jnp.int32) * requests + device_index
    destination = jnp.sum((request_ends[None, :] <= group_index[:, None]).astype(jnp.int32), axis=1)
    owned_start = jnp.sum(
        jnp.where(destination[:, None] == request_ids[None, :], starts[None, :], 0), axis=1
    )
    target = destination * capacity + (group_index - owned_start) // requests
    usable = destination < requests
    send_slots = jnp.arange(requests * capacity, dtype=jnp.int32)
    placing = ((send_slots[:, None] == target[None, :]) & usable[None, :]).astype(jnp.bfloat16)
    outgoing = jnp.dot(placing, merged, preferred_element_type=jnp.float32).astype(jnp.bfloat16)
    arrived = lax.all_to_all(
        outgoing.reshape(requests, capacity, feature_width),
        "req",
        split_axis=0,
        concat_axis=0,
        tiled=True,
    )
    arrived = arrived.reshape(requests * capacity, feature_width)
    own_request = request_ids == device_index
    own_count = jnp.sum(jnp.where(own_request, counts, 0))
    own_start = jnp.sum(jnp.where(own_request, starts, 0))
    image_from = image_at[0]
    prompt_count = prompt_len[0]
    seq_slots = prompt.shape[1] + IMG_MAX
    slot_index = jnp.arange(seq_slots, dtype=jnp.int32)
    image_row = slot_index - image_from
    in_image = (image_row >= 0) & (image_row < own_count)
    is_live = slot_index < prompt_count + own_count
    from_prompt = is_live & jnp.logical_not(in_image)
    flat_index = (own_start + image_row) % requests * capacity + image_row // requests
    image_pick = ((flat_index[:, None] == send_slots[None, :]) & in_image[:, None]).astype(
        jnp.bfloat16
    )
    prompt_row = jnp.where(slot_index < image_from, slot_index, slot_index - own_count)
    prompt_ids = jnp.arange(prompt.shape[1], dtype=jnp.int32)
    prompt_pick = ((prompt_row[:, None] == prompt_ids[None, :]) & from_prompt[:, None]).astype(
        jnp.bfloat16
    )
    embedded = (
        jnp.dot(image_pick, arrived, preferred_element_type=jnp.float32)
        + jnp.dot(prompt_pick, prompt[0], preferred_element_type=jnp.float32)
    ).astype(jnp.bfloat16)
    values = embedded.astype(jnp.float32)
    square_sum = lax.psum(jnp.sum(values * values, axis=-1, keepdims=True), "tp")
    mean_square = square_sum / (feature_width * lax.axis_size("tp"))
    own_gain = lax.dynamic_slice_in_dim(norm_gain, tp_index * feature_width, feature_width, 0)
    normed = (values * lax.rsqrt(mean_square + 1e-05) * own_gain[None, :]).astype(jnp.bfloat16)
    normed = lax.all_gather(normed, "req", axis=0, axis_index_groups=in_plane, tiled=True)
    normed = lax.all_gather(normed, "tp", axis=1, tiled=True)
    projected = jnp.dot(normed, decoder_weight, preferred_element_type=jnp.float32)
    cosine_table, sine_table = rope_tables(seq_slots)
    cosine_table = jnp.tile(cosine_table, (plane, 1))
    sine_table = jnp.tile(sine_table, (plane, 1))
    turned = apply_rope(projected, cosine_table, sine_table).astype(jnp.bfloat16)
    turned = lax.all_to_all(
        turned.reshape(plane, seq_slots, -1),
        "req",
        split_axis=0,
        concat_axis=0,
        axis_index_groups=in_plane,
        tiled=True,
    )
    return jnp.swapaxes(turned, 0, 1).reshape(seq_slots, -1)


MESH = pl.DeviceIdType.MESH
BF16 = jnp.bfloat16
F32 = jnp.float32


def dot(a, b):
    return jnp.dot(a, b, preferred_element_type=F32)


def fused_kernel(
    dims,
    context,
    residual,
    out_weight,
    scale,
    prompt,
    gain,
    qkv_weight,
    target_row,
    image_from,
    slot_from,
    cosine,
    sine,
    out,
    slab,
    out_slab,
    blocks,
    partials,
    returned,
    mean_residual,
    merged,
    outgoing,
    arrived,
    images,
    squares,
    image_squares,
    texts,
    pictures,
    sources,
    total,
    turned,
    assembled,
    slab_in_send,
    slab_in_recv,
    slab_local,
    slab_send,
    slab_recv,
    out_slab_send,
    out_slab_recv,
    out_slab_local,
    block_send,
    block_recv,
    partial_send,
    partial_recv,
    place_send,
    place_recv,
    square_send,
    square_recv,
    text_send,
    text_recv,
    text_cross,
    picture_send,
    picture_recv,
    picture_cross,
    source_send,
    source_recv,
    turned_send,
    turned_recv,
    turned_local,
    slab_far_send,
    slab_far_recv,
    block_far_send,
    block_far_recv,
):
    requests, cores, plane, depth = dims
    req = lax.axis_index("req")
    core = lax.axis_index("tp")
    level = req // plane
    spot = req % plane
    sibling = 1 - core
    rows = blocks.shape[1]
    width = blocks.shape[2]
    depth_rows = qkv_weight.shape[0]
    share = slab.shape[-1]
    columns = out_weight.shape[1]
    seq = out.shape[0]
    half = width // 2
    held = depth // cores
    others = [
        ((spot // 2 + ry) % 2) * 2 + (spot % 2 + rx) % 2 for ry, rx in ((0, 1), (1, 0), (1, 1))
    ]

    def remote(src, dst, send, recv, to_req, to_core):
        return pltpu.make_async_remote_copy(
            src_ref=src,
            dst_ref=dst,
            send_sem=send,
            recv_sem=recv,
            device_id=(to_req, to_core),
            device_id_type=MESH,
        )

    def arrive(dst, recv):
        remote(dst, dst, slab_local, recv, req, sibling).wait_recv()

    barrier = pltpu.get_barrier_semaphore()
    count = requests * cores

    @pl.loop(1, count)
    def _(offset):
        at = (req * cores + core + offset) % count
        pl.semaphore_signal(
            barrier, inc=1, device_id=(at // cores, at % cores), device_id_type=MESH
        )

    pl.semaphore_wait(barrier, count - 1)

    slab_sends = []
    for i, other in enumerate(others):
        at = pl.multiple_of(other * share, share)
        slab_sends.append(
            remote(
                qkv_weight.at[:, pl.ds(at, share)],
                slab.at[level, spot],
                slab_in_send.at[i],
                slab_in_recv.at[spot],
                level * plane + other,
                core,
            )
        )
        slab_sends[-1].start()
    slab_own = pltpu.make_async_copy(
        qkv_weight.at[:, pl.ds(pl.multiple_of(spot * share, share), share)],
        slab.at[level, spot],
        slab_local,
    )
    slab_own.start()

    out_sends = []
    for i, other in enumerate(others):
        out_sends.append(
            remote(
                out_weight,
                out_slab.at[spot],
                out_slab_send.at[i],
                out_slab_recv.at[spot],
                level * plane + other,
                core,
            )
        )
        out_sends[-1].start()
    out_own = pltpu.make_async_copy(out_weight, out_slab.at[spot], out_slab_local)
    out_own.start()

    first_patch = 4 * lax.broadcasted_iota(jnp.int32, (rows, 4 * rows), 0)
    patch = lax.broadcasted_iota(jnp.int32, (rows, 4 * rows), 1)
    inside = (patch >= first_patch) & (patch < first_patch + 4)
    averaging = jnp.where(inside, 0.25, 0.0).astype(BF16)
    for i in range(width // 512):
        cols = slice(i * 512, (i + 1) * 512)
        blocks[level, :, cols] = dot(averaging, context[:, cols]).astype(BF16)

    def hand(part, send, recv, to_level):
        return remote(part, part, send, recv, to_level * plane + spot, core)

    def near_copies(buffer, send, recv):
        own = buffer.at[level]
        for d in (1, 2):
            yield level + d < depth, hand(own, send.at[d - 1, 0], recv.at[level], level + d)
            yield level - d >= 0, hand(own, send.at[d - 1, 1], recv.at[level], level - d)

    def near_start(buffer, send, recv):
        for there, copy in near_copies(buffer, send, recv):
            pl.when(there)(copy.start)

    def near_sent(buffer, send, recv):
        for there, copy in near_copies(buffer, send, recv):
            pl.when(there)(copy.wait_send)

    def hop_copies(buffer, send, recv, hop):
        up, down = level + 1 < depth, level - 1 >= 0
        if hop == 1:
            own = buffer.at[level]
            yield up, hand(own, send.at[0, 0], recv.at[level], level + 1)
            yield down, hand(own, send.at[0, 1], recv.at[level], level - 1)
        else:
            below, above = buffer.at[level - 1], buffer.at[level + 1]
            yield up & down, hand(below, send.at[1, 0], recv.at[level - 1], level + 1)
            yield up & down, hand(above, send.at[1, 1], recv.at[level + 1], level - 1)

    def hop_start(buffer, send, recv, hop):
        for there, copy in hop_copies(buffer, send, recv, hop):
            pl.when(there)(copy.start)

    def hop_sent(buffer, send, recv):
        for hop in (1, 2):
            for there, copy in hop_copies(buffer, send, recv, hop):
                pl.when(there)(copy.wait_send)

    def far_copies(buffer, send, far_recv):
        pieces = far_recv.shape[0]
        size = buffer.shape[-1] // pieces
        for here, at, to in ((2, 0, 3), (1, 3, 0)):
            for i in range(pieces):
                part = buffer.at[at, ..., pl.ds(i * size, size)]
                yield level == here, hand(part, send.at[i], far_recv.at[i], to)

    def far_start(buffer, recv, send, far_recv):
        @pl.when(level == 2)
        def _():
            arrive(buffer.at[0], recv.at[0])

        @pl.when(level == 1)
        def _():
            arrive(buffer.at[3], recv.at[3])

        for there, copy in far_copies(buffer, send, far_recv):
            pl.when(there)(copy.start)

    def far_sent(buffer, send, far_recv):
        for there, copy in far_copies(buffer, send, far_recv):
            pl.when(there)(copy.wait_send)

    def near_arrive(buffer, recv, d):
        @pl.when((level - d >= 0) & ((d == 1) | (level == 3)))
        def _():
            arrive(buffer.at[level - d], recv.at[level - d])

        @pl.when((level + d < depth) & ((d == 1) | (level == 0)))
        def _():
            arrive(buffer.at[level + d], recv.at[level + d])

    def far_arrive(buffer, far_recv, i):
        size = buffer.shape[-1] // far_recv.shape[0]
        for here, at in ((0, 3), (3, 0)):

            @pl.when(level == here)
            def _():
                arrive(buffer.at[at, ..., pl.ds(i * size, size)], far_recv.at[i])

    near_start(blocks, block_send, block_recv)

    for i in range(width // 512):
        cols = slice(i * 512, (i + 1) * 512)
        mean_residual[:, cols] = dot(averaging, residual[:, cols])

    own_gain = gain[:, pl.ds(pl.multiple_of(core * width, width), width)]

    def squares_of(values):
        return jnp.broadcast_to(
            jnp.sum(values * values, axis=-1, keepdims=True), (values.shape[0], 128)
        )

    def share_squares(buffer, i):
        copy = remote(
            buffer.at[0], buffer.at[1], square_send.at[i], square_recv.at[i], req, sibling
        )
        copy.start()
        copy.wait()
        mean_square = (buffer[0, :, :1] + buffer[1, :, :1]) / (width * cores)
        return lax.rsqrt(mean_square + 1e-05)

    squares[0] = squares_of(prompt[...].astype(F32))
    factor = share_squares(squares, 0)
    for i in range(width // 512):
        cols = slice(i * 512, (i + 1) * 512)
        texts[spot, core, :, cols] = (
            prompt[:, cols].astype(F32) * factor * own_gain[:, cols]
        ).astype(BF16)
    sources[spot] = jnp.broadcast_to(slot_from[...], sources.shape[1:]).astype(BF16)

    far_start(blocks, block_recv, block_far_send, block_far_recv)
    near_arrive(blocks, block_recv, 1)
    near_arrive(blocks, block_recv, 2)
    far_arrive(blocks, block_far_recv, 0)

    slab_own.wait()
    for other in others:
        arrive(slab.at[level, other], slab_in_recv.at[other])
    hop_start(slab, slab_send, slab_recv, 1)

    out_own.wait()
    for other in others:
        arrive(out_slab.at[other], out_slab_recv.at[other])

    def part_of(buffer, place, part, i):
        if i is None:
            return buffer.at[place, part]
        size = buffer.shape[2] // 2
        return buffer.at[place, part, pl.ds(i * size, size)]

    def spread(half_index, buffer, send, recv):
        copies = []
        for i, other in enumerate(others):
            own = part_of(buffer, spot, core, half_index)
            copies.append(
                remote(own, own, send.at[i], recv.at[spot, core], level * plane + other, core)
            )
            copies[-1].start()
        return copies

    def cross(half_index, buffer, place, send, recv):
        part = part_of(buffer, place, core, half_index)
        copy = remote(part, part, send, recv.at[place, core], req, sibling)
        copy.start()
        return copy

    sends = []
    for i, other in enumerate(others):
        own = sources.at[spot]
        sends.append(
            remote(
                own, own, source_send.at[i], source_recv.at[spot], level * plane + other, core
            )
        )
        sends[-1].start()
    sends.extend(spread(0, texts, text_send.at[0], text_recv.at[0]))

    owner_core = level // held
    lane = level % held

    @pl.loop(0, depth)
    def _(step):
        target = (level + 1 + step) % depth
        for i in range(plane):
            partials[target, :, i * columns : (i + 1) * columns] = dot(
                blocks[target], out_slab[i]
            ).astype(BF16)
        own = (target == level) & (owner_core == core)

        @pl.when(own)
        def _():
            pltpu.make_async_copy(
                partials.at[target], returned.at[lane, core], partial_recv.at[lane, core]
            ).start()

        @pl.when(jnp.logical_not(own))
        def _():
            remote(
                partials.at[target],
                returned.at[lane, core],
                partial_send.at[target],
                partial_recv.at[lane, core],
                target * plane + spot,
                owner_core,
            ).start()

    for i in range(held):
        for j in range(cores):
            arrive(returned.at[i, j], partial_recv.at[i, j])
    for i in range(held):
        cols = slice(i * half, (i + 1) * half)
        added = returned[i, 0].astype(F32)
        for j in range(1, cores):
            added = added + returned[i, j].astype(F32)
        merged[:, cols] = (mean_residual[:, cols] + scale[:, cols] * added).astype(BF16)

    block_rows = outgoing.shape[1]
    slot = lax.broadcasted_iota(jnp.int32, (requests * block_rows, rows), 0)
    placed = jnp.zeros((requests * block_rows, half), F32)
    for i in range(2):
        place = jnp.where(slot == target_row[...] + i * (block_rows // 2), 1.0, 0.0).astype(BF16)
        placed = placed + dot(place, merged[:, i * half : (i + 1) * half])
    outgoing[...] = placed.astype(BF16).reshape(outgoing.shape)

    @pl.loop(1, requests)
    def _(offset):
        to = (req + offset) % requests
        remote(
            outgoing.at[to], arrived.at[req], place_send.at[to], place_recv.at[req], to, core
        ).start()

    place_own = pltpu.make_async_copy(outgoing.at[req], arrived.at[req], place_send.at[req])
    place_own.start()
    near_arrive(slab, slab_recv, 1)
    hop_start(slab, slab_send, slab_recv, 2)
    place_own.wait()

    @pl.loop(1, requests)
    def _(offset):
        source = (req + offset) % requests
        arrive(arrived.at[source], place_recv.at[source])

    slot = lax.broadcasted_iota(jnp.int32, (images.shape[0], requests * block_rows), 1)
    for i in range(2):
        pick = jnp.where(slot == image_from[...] + i * (block_rows // 2), 1.0, 0.0).astype(BF16)
        images[:, i * half : (i + 1) * half] = dot(
            pick, arrived[...].reshape(requests * block_rows, half)
        )
    image_squares[0] = squares_of(images[...])
    factor = share_squares(image_squares, 1)
    for i in range(2):
        cols = slice(i * half, (i + 1) * half)
        pictures[spot, core, :, cols] = (images[:, cols] * factor * own_gain[:, cols]).astype(BF16)
    sends.extend(spread(None, pictures, picture_send, picture_recv))
    sends.extend(spread(1, texts, text_send.at[1], text_recv.at[1]))
    sends.append(cross(None, pictures, spot, picture_cross.at[0], picture_recv))
    for h in range(2):
        sends.append(cross(h, texts, spot, text_cross.at[h, 0], text_recv.at[h]))
    far_start(slab, slab_recv, slab_far_send, slab_far_recv)

    def hand_over(h, buffer, send, recv):
        for i, other in enumerate(others):
            arrive(part_of(buffer, other, core, h), recv.at[other, core])
            sends.append(cross(h, buffer, other, send.at[i + 1], recv))

    for other in others:
        arrive(sources.at[other], source_recv.at[other])
    hand_over(0, texts, text_cross.at[0], text_recv.at[0])
    hand_over(None, pictures, picture_cross, picture_recv)
    hand_over(1, texts, text_cross.at[1], text_recv.at[1])
    for place in [spot] + others:
        for h in range(2):
            arrive(part_of(texts, place, sibling, h), text_recv.at[h, place, sibling])
        arrive(pictures.at[place, sibling], picture_recv.at[place, sibling])

    tile = 256
    level_rows = plane * depth_rows
    seq_texts = texts.shape[2]
    lanes = lax.broadcasted_iota(jnp.int32, (seq, 128), 1).astype(F32)

    def level_of(at, place):
        part = at // held
        base = pl.multiple_of((at % held) * level_rows, level_rows)
        source = sources[place].astype(F32)
        picks = [
            jnp.where(source == lanes + i * 128, 1.0, 0.0).astype(BF16)
            for i in range(seq_texts // 128)
        ]
        image_pick = jnp.where(source == -1.0 - lanes, 1.0, 0.0).astype(BF16)
        text_pick = jnp.concatenate(picks, axis=1)
        a = dot(text_pick, texts[place, part, :, pl.ds(base, level_rows)]) + dot(
            image_pick, pictures[place, part, :, pl.ds(base, level_rows)]
        )
        return a.astype(BF16)

    def multiply_all(at, first):
        @pl.loop(0, plane)
        def _(place):
            a = level_of(at, place)
            for n in range(share // tile):
                cols = slice(n * tile, (n + 1) * tile)
                b = slab[at, :, :, cols].reshape(level_rows, tile)
                if first:
                    total[place, :, cols] = dot(a, b)
                else:
                    total[place, :, cols] += dot(a, b)

    multiply_all(level, True)
    for d in (1, 2):
        if d == 2:
            near_arrive(slab, slab_recv, d)

        @pl.when(level - d >= 0)
        def _():
            multiply_all(level - d, False)

        @pl.when(level + d < depth)
        def _():
            multiply_all(level + d, False)

    at_edge = (level == 0) | (level == depth - 1)
    last = depth - 1 - level

    @pl.when(at_edge)
    def _():
        @pl.loop(0, plane)
        def _(place):
            assembled[place] = level_of(last, place)

    def leave(place, n):
        start = pl.multiple_of(spot * share + n * tile, tile)
        return remote(
            turned.at[place, :, pl.ds(n * tile, tile)],
            out.at[:, pl.ds(start, tile)],
            turned_send.at[place, n],
            turned_recv.at[spot, n],
            level * plane + place,
            core,
        )

    for n in range(share // tile):
        far_arrive(slab, slab_far_recv, n)

        @pl.loop(0, plane)
        def _(step):
            place = (spot + 1 + step) % plane

            @pl.when(at_edge)
            def _():
                cols = slice(n * tile, (n + 1) * tile)
                b = slab[last, :, :, cols].reshape(level_rows, tile)
                total[place, :, cols] += dot(assembled[place], b)

            for head in range(n * tile // HEAD, (n + 1) * tile // HEAD):
                cols = slice(head * HEAD, (head + 1) * HEAD)
                values = total[place, :, cols]
                if head <= GROUP:
                    values = values * cosine[...] + pltpu.roll(values, HEAD // 2, 1) * sine[...]
                turned[place, :, cols] = values.astype(BF16)

            @pl.when(step < plane - 1)
            def _():
                leave(place, n).start()

    here = pl.ds(pl.multiple_of(spot * share, share), share)
    turned_own = pltpu.make_async_copy(turned.at[spot], out.at[:, here], turned_local)
    turned_own.start()

    for copy in out_sends + slab_sends + sends:
        copy.wait_send()
    near_sent(blocks, block_send, block_recv)
    far_sent(blocks, block_far_send, block_far_recv)
    hop_sent(slab, slab_send, slab_recv)
    far_sent(slab, slab_far_send, slab_far_recv)

    @pl.loop(0, depth)
    def _(target):
        @pl.when(jnp.logical_not((target == level) & (owner_core == core)))
        def _():
            remote(
                partials.at[target],
                returned.at[lane, core],
                partial_send.at[target],
                partial_recv.at[lane, core],
                req,
                sibling,
            ).wait_send()

    @pl.loop(1, requests)
    def _(offset):
        to = (req + offset) % requests
        remote(
            outgoing.at[to], arrived.at[req], place_send.at[to], place_recv.at[req], req, sibling
        ).wait_send()

    for other in others:
        for n in range(share // tile):
            leave(other, n).wait_send()
    turned_own.wait()
    for other in others:
        for n in range(share // tile):
            start = pl.multiple_of(other * share + n * tile, tile)
            arrive(out.at[:, pl.ds(start, tile)], turned_recv.at[other, n])


def fused_shards(
    vit_context,
    vision_residual,
    out_weight,
    layer_scale,
    prompt,
    prompt_len,
    image_at,
    grid_sizes,
    image_owner,
    norm_gain,
    qkv_weight,
):
    requests = lax.axis_size("req")
    cores = lax.axis_size("tp")
    device_index = lax.axis_index("req")
    tp_index = lax.axis_index("tp")
    patches, width = vit_context.shape
    rows = patches // 4
    share = (GROUP + 2) * HEAD
    plane = qkv_weight.shape[1] // share
    depth = requests // plane
    seq_slots = prompt.shape[1] + IMG_MAX

    counts, starts = request_plan(grid_sizes, image_owner, requests)
    request_ends = starts + counts
    capacity = (IMG_MAX + requests - 1) // requests
    request_ids = jnp.arange(requests, dtype=jnp.int32)
    group_index = jnp.arange(rows, dtype=jnp.int32) * requests + device_index
    destination = jnp.sum((request_ends[None, :] <= group_index[:, None]).astype(jnp.int32), axis=1)
    owned_start = jnp.sum(
        jnp.where(destination[:, None] == request_ids[None, :], starts[None, :], 0), axis=1
    )
    target = destination * 2 * capacity + (group_index - owned_start) // requests
    usable = destination < requests
    target = jnp.where(usable, target, -requests * 2 * capacity)
    own_request = request_ids == device_index
    own_count = jnp.sum(jnp.where(own_request, counts, 0))
    own_start = jnp.sum(jnp.where(own_request, starts, 0))
    image_from = image_at[0]
    prompt_count = prompt_len[0]
    image_row = jnp.arange(IMG_MAX, dtype=jnp.int32)
    from_flat = (own_start + image_row) % requests * 2 * capacity + image_row // requests
    from_flat = jnp.where(image_row < own_count, from_flat, -requests * 2 * capacity)
    slot_index = jnp.arange(seq_slots, dtype=jnp.int32)
    slot_image = slot_index - image_from
    in_image = (slot_image >= 0) & (slot_image < own_count)
    slot_row = jnp.where(slot_index < image_from, slot_index, slot_index - own_count)
    slot_from = jnp.where(slot_index < prompt_count + own_count, slot_row, 512)
    slot_from = jnp.where(in_image, -1 - slot_image, slot_from)
    cosine_table, sine_table = rope_tables(seq_slots)
    cosine = jnp.concatenate([cosine_table, cosine_table], axis=1)
    sine = jnp.concatenate([-sine_table, sine_table], axis=1)

    vmem = pl.BlockSpec(memory_space=pltpu.VMEM)
    anywhere = pl.BlockSpec(memory_space=pl.ANY)
    dma = pltpu.SemaphoreType.DMA
    columns = out_weight.shape[1]
    half = width // 2
    return pl.pallas_call(
        functools.partial(fused_kernel, (requests, cores, plane, depth)),
        out_shape=jax.ShapeDtypeStruct((seq_slots, qkv_weight.shape[1]), BF16),
        in_specs=[vmem, vmem, anywhere, vmem, vmem, vmem, anywhere] + [vmem] * 5,
        out_specs=anywhere,
        scratch_shapes=[
            pltpu.VMEM((depth, plane, qkv_weight.shape[0], share), BF16),
            pltpu.VMEM((plane, width, columns), BF16),
            pltpu.VMEM((depth, rows, width), BF16),
            pltpu.VMEM((depth, rows, plane * columns), BF16),
            pltpu.VMEM((depth // cores, cores, rows, plane * columns), BF16),
            pltpu.VMEM((rows, width), F32),
            pltpu.VMEM((rows, width), BF16),
            pltpu.VMEM((requests, 2 * capacity, half), BF16),
            pltpu.VMEM((requests, 2 * capacity, half), BF16),
            pltpu.VMEM((IMG_MAX, width), F32),
            pltpu.VMEM((2, prompt.shape[1], 128), F32),
            pltpu.VMEM((2, IMG_MAX, 128), F32),
            pltpu.VMEM((plane, cores, prompt.shape[1], width), BF16),
            pltpu.VMEM((plane, cores, IMG_MAX, width), BF16),
            pltpu.VMEM((plane, seq_slots, 128), BF16),
            pltpu.VMEM((plane, seq_slots, share), F32),
            pltpu.VMEM((plane, seq_slots, share), BF16),
            pltpu.VMEM((plane, seq_slots, plane * qkv_weight.shape[0]), BF16),
            dma((plane,)),
            dma((plane,)),
            dma,
            dma((depth, 2)),
            dma((depth,)),
            dma((plane,)),
            dma((plane,)),
            dma,
            dma((depth, 2)),
            dma((depth,)),
            dma((depth,)),
            dma((depth // cores, cores)),
            dma((requests,)),
            dma((requests,)),
            dma((2,)),
            dma((2,)),
            dma((2, plane)),
            dma((2, plane, cores)),
            dma((2, plane)),
            dma((plane,)),
            dma((plane, cores)),
            dma((plane,)),
            dma((plane,)),
            dma((plane,)),
            dma((plane, 3)),
            dma((plane, 3)),
            dma,
            dma((3,)),
            dma((3,)),
            dma((1,)),
            dma((1,)),
        ],
        compiler_params=pltpu.CompilerParams(
            collective_id=0, has_side_effects=True, vmem_limit_bytes=58 * 1024 * 1024
        ),
        cost_estimate=pl.CostEstimate(
            flops=30 * 10**9, bytes_accessed=20 * 2**20, transcendentals=0
        ),
    )(
        vit_context,
        vision_residual,
        out_weight,
        layer_scale[None, :],
        prompt[0],
        norm_gain[None, :],
        qkv_weight,
        target[None, :],
        from_flat[:, None],
        slot_from[:, None],
        cosine,
        sine,
    )


def solution(mesh):
    requests, cores = mesh.shape["req"], mesh.shape["tp"]

    def shards(*arrays):
        patches, width = arrays[0].shape
        plane = arrays[-1].shape[1] // ((GROUP + 2) * HEAD)
        fits = (
            cores == 2
            and plane == 4
            and requests // plane == 4
            and arrays[2].shape[1] * requests == width * cores
            and arrays[2].shape[1] % 128 == 0
            and IMG_MAX % requests == 0
            and (IMG_MAX // requests) % 8 == 0
            and IMG_MAX == 128
            and arrays[4].shape[1] in (128, 256)
        )
        return (fused_shards if fits else collective_shards)(*arrays)

    in_specs = (
        P("req", "tp"),
        P("req", "tp"),
        P("tp", "req"),
        P("tp"),
        P("req", None, "tp"),
        P("req"),
        P("req"),
        P(),
        P(),
        P(),
        P("req", "tp"),
    )
    out_specs = P("req", "tp")
    return jax.shard_map(shards, mesh=mesh, in_specs=in_specs, out_specs=out_specs, check_vma=False)
```

```python
import functools

import jax
import jax.numpy as jnp
from jax import lax
from jax.experimental import pallas as pl
from jax.experimental.pallas import tpu as pltpu
from jax.sharding import PartitionSpec as P

HEAD = 128
GROUP = 4
IMG_MAX = 128


def request_plan(grid_sizes, image_owner, requests):
    image_rows = grid_sizes[:, 0] * grid_sizes[:, 1]
    member = (image_owner[:, None] == jnp.arange(requests, dtype=jnp.int32)[None, :]).astype(
        jnp.int32
    )
    counts = jnp.sum(image_rows[:, None] * member, axis=0)
    starts = jnp.cumsum(counts) - counts
    return (counts, starts)


def rope_tables(count):
    half_size = HEAD // 2
    exponent = jnp.arange(half_size, dtype=jnp.float32) * (2.0 / HEAD)
    frequency = jnp.exp(-exponent * jnp.log(jnp.float32(500000.0)))
    angles = jnp.arange(count, dtype=jnp.float32)[:, None] * frequency[None, :]
    return (jnp.cos(angles), jnp.sin(angles))


def apply_rope(projected, cosine_table, sine_table):
    seq_rows = projected.shape[0]
    head_blocks = projected.reshape(seq_rows, -1, GROUP + 2, HEAD)
    turning = head_blocks[:, :, : GROUP + 1, :]
    first_half = turning[..., : HEAD // 2]
    second_half = turning[..., HEAD // 2 :]
    cosine_wide = cosine_table[:, None, None, :]
    sine_wide = sine_table[:, None, None, :]
    turned = jnp.concatenate(
        [
            first_half * cosine_wide - second_half * sine_wide,
            second_half * cosine_wide + first_half * sine_wide,
        ],
        axis=-1,
    )
    head_blocks = jnp.concatenate([turned, head_blocks[:, :, GROUP + 1 :, :]], axis=2)
    return head_blocks.reshape(seq_rows, -1)


def collective_shards(
    vit_context,
    vision_residual,
    out_weight,
    layer_scale,
    prompt,
    prompt_len,
    image_at,
    grid_sizes,
    image_owner,
    norm_gain,
    qkv_weight,
):
    requests = lax.axis_size("req")
    device_index = lax.axis_index("req")
    tp_index = lax.axis_index("tp")
    feature_width = vit_context.shape[1]
    plane = qkv_weight.shape[1] // ((GROUP + 2) * HEAD)
    depth = requests // plane
    in_plane = [[d * plane + i for i in range(plane)] for d in range(depth)]
    in_depth = [[d * plane + i for d in range(depth)] for i in range(plane)]
    weight_rows = qkv_weight.shape[0]
    weight_parts = jnp.swapaxes(qkv_weight.reshape(weight_rows, plane, -1), 0, 1)
    weight_parts = lax.all_to_all(
        weight_parts, "req", split_axis=0, concat_axis=0, axis_index_groups=in_plane, tiled=True
    )
    decoder_weight = lax.all_gather(
        weight_parts.reshape(plane * weight_rows, -1),
        "req",
        axis=0,
        axis_index_groups=in_depth,
        tiled=True,
    )
    merged_context = jnp.mean(
        vit_context.astype(jnp.float32).reshape(-1, 4, feature_width), axis=1
    ).astype(jnp.bfloat16)
    merged_residual = jnp.mean(
        vision_residual.astype(jnp.float32).reshape(-1, 4, feature_width), axis=1
    )
    partial_value = jnp.dot(
        lax.all_gather(merged_context, "req", axis=0, axis_index_groups=in_depth, tiled=True),
        lax.all_gather(out_weight, "req", axis=1, axis_index_groups=in_plane, tiled=True),
        preferred_element_type=jnp.float32,
    )
    returned = lax.all_to_all(
        partial_value.astype(jnp.bfloat16).reshape(depth, merged_context.shape[0], -1),
        "req",
        split_axis=0,
        concat_axis=0,
        axis_index_groups=in_depth,
        tiled=True,
    )
    returned = jnp.swapaxes(returned, 0, 1).reshape(merged_context.shape[0], -1)
    summed = lax.psum(returned, "tp").astype(jnp.float32)
    own_share = lax.dynamic_slice_in_dim(summed, tp_index * feature_width, feature_width, 1)
    merged = (merged_residual + layer_scale[None, :] * own_share).astype(jnp.bfloat16)
    merged_count = merged.shape[0]
    counts, starts = request_plan(grid_sizes, image_owner, requests)
    request_ends = starts + counts
    capacity = (IMG_MAX + requests - 1) // requests
    request_ids = jnp.arange(requests, dtype=jnp.int32)
    group_index = jnp.arange(merged_count, dtype=jnp.int32) * requests + device_index
    destination = jnp.sum((request_ends[None, :] <= group_index[:, None]).astype(jnp.int32), axis=1)
    owned_start = jnp.sum(
        jnp.where(destination[:, None] == request_ids[None, :], starts[None, :], 0), axis=1
    )
    target = destination * capacity + (group_index - owned_start) // requests
    usable = destination < requests
    send_slots = jnp.arange(requests * capacity, dtype=jnp.int32)
    placing = ((send_slots[:, None] == target[None, :]) & usable[None, :]).astype(jnp.bfloat16)
    outgoing = jnp.dot(placing, merged, preferred_element_type=jnp.float32).astype(jnp.bfloat16)
    arrived = lax.all_to_all(
        outgoing.reshape(requests, capacity, feature_width),
        "req",
        split_axis=0,
        concat_axis=0,
        tiled=True,
    )
    arrived = arrived.reshape(requests * capacity, feature_width)
    own_request = request_ids == device_index
    own_count = jnp.sum(jnp.where(own_request, counts, 0))
    own_start = jnp.sum(jnp.where(own_request, starts, 0))
    image_from = image_at[0]
    prompt_count = prompt_len[0]
    seq_slots = prompt.shape[1] + IMG_MAX
    slot_index = jnp.arange(seq_slots, dtype=jnp.int32)
    image_row = slot_index - image_from
    in_image = (image_row >= 0) & (image_row < own_count)
    is_live = slot_index < prompt_count + own_count
    from_prompt = is_live & jnp.logical_not(in_image)
    flat_index = (own_start + image_row) % requests * capacity + image_row // requests
    image_pick = ((flat_index[:, None] == send_slots[None, :]) & in_image[:, None]).astype(
        jnp.bfloat16
    )
    prompt_row = jnp.where(slot_index < image_from, slot_index, slot_index - own_count)
    prompt_ids = jnp.arange(prompt.shape[1], dtype=jnp.int32)
    prompt_pick = ((prompt_row[:, None] == prompt_ids[None, :]) & from_prompt[:, None]).astype(
        jnp.bfloat16
    )
    embedded = (
        jnp.dot(image_pick, arrived, preferred_element_type=jnp.float32)
        + jnp.dot(prompt_pick, prompt[0], preferred_element_type=jnp.float32)
    ).astype(jnp.bfloat16)
    values = embedded.astype(jnp.float32)
    square_sum = lax.psum(jnp.sum(values * values, axis=-1, keepdims=True), "tp")
    mean_square = square_sum / (feature_width * lax.axis_size("tp"))
    own_gain = lax.dynamic_slice_in_dim(norm_gain, tp_index * feature_width, feature_width, 0)
    normed = (values * lax.rsqrt(mean_square + 1e-05) * own_gain[None, :]).astype(jnp.bfloat16)
    normed = lax.all_gather(normed, "req", axis=0, axis_index_groups=in_plane, tiled=True)
    normed = lax.all_gather(normed, "tp", axis=1, tiled=True)
    projected = jnp.dot(normed, decoder_weight, preferred_element_type=jnp.float32)
    cosine_table, sine_table = rope_tables(seq_slots)
    cosine_table = jnp.tile(cosine_table, (plane, 1))
    sine_table = jnp.tile(sine_table, (plane, 1))
    turned = apply_rope(projected, cosine_table, sine_table).astype(jnp.bfloat16)
    turned = lax.all_to_all(
        turned.reshape(plane, seq_slots, -1),
        "req",
        split_axis=0,
        concat_axis=0,
        axis_index_groups=in_plane,
        tiled=True,
    )
    return jnp.swapaxes(turned, 0, 1).reshape(seq_slots, -1)


MESH = pl.DeviceIdType.MESH
BF16 = jnp.bfloat16
F32 = jnp.float32


def dot(a, b):
    return jnp.dot(a, b, preferred_element_type=F32)


def fused_kernel(
    dims,
    context,
    residual,
    out_weight,
    scale,
    prompt,
    gain,
    qkv_weight,
    target_row,
    image_from,
    slot_from,
    cosine,
    sine,
    out,
    slab,
    out_slab,
    blocks,
    partials,
    returned,
    mean_residual,
    merged,
    outgoing,
    arrived,
    images,
    squares,
    image_squares,
    texts,
    pictures,
    sources,
    total,
    turned,
    assembled,
    slab_in_send,
    slab_in_recv,
    slab_local,
    slab_send,
    slab_recv,
    out_slab_send,
    out_slab_recv,
    out_slab_local,
    block_send,
    block_recv,
    partial_send,
    partial_recv,
    place_send,
    place_recv,
    square_send,
    square_recv,
    text_send,
    text_recv,
    text_cross,
    picture_send,
    picture_recv,
    picture_cross,
    source_send,
    source_recv,
    turned_send,
    turned_recv,
    turned_local,
    slab_far_send,
    slab_far_recv,
    block_far_send,
    block_far_recv,
):
    requests, cores, plane, depth = dims
    req = lax.axis_index("req")
    core = lax.axis_index("tp")
    level = req // plane
    spot = req % plane
    sibling = 1 - core
    rows = blocks.shape[1]
    width = blocks.shape[2]
    depth_rows = qkv_weight.shape[0]
    share = slab.shape[-1]
    columns = out_weight.shape[1]
    seq = out.shape[0]
    half = width // 2
    held = depth // cores
    others = [
        ((spot // 2 + ry) % 2) * 2 + (spot % 2 + rx) % 2 for ry, rx in ((0, 1), (1, 0), (1, 1))
    ]

    def remote(src, dst, send, recv, to_req, to_core):
        return pltpu.make_async_remote_copy(
            src_ref=src,
            dst_ref=dst,
            send_sem=send,
            recv_sem=recv,
            device_id=(to_req, to_core),
            device_id_type=MESH,
        )

    def arrive(dst, recv):
        remote(dst, dst, slab_local, recv, req, sibling).wait_recv()

    barrier = pltpu.get_barrier_semaphore()
    count = requests * cores

    @pl.loop(1, count)
    def _(offset):
        at = (req * cores + core + offset) % count
        pl.semaphore_signal(
            barrier, inc=1, device_id=(at // cores, at % cores), device_id_type=MESH
        )

    pl.semaphore_wait(barrier, count - 1)

    slab_sends = []
    for i, other in enumerate(others):
        at = pl.multiple_of(other * share, share)
        slab_sends.append(
            remote(
                qkv_weight.at[:, pl.ds(at, share)],
                slab.at[level, spot],
                slab_in_send.at[i],
                slab_in_recv.at[spot],
                level * plane + other,
                core,
            )
        )
        slab_sends[-1].start()
    slab_own = pltpu.make_async_copy(
        qkv_weight.at[:, pl.ds(pl.multiple_of(spot * share, share), share)],
        slab.at[level, spot],
        slab_local,
    )
    slab_own.start()

    out_sends = []
    for i, other in enumerate(others):
        out_sends.append(
            remote(
                out_weight,
                out_slab.at[spot],
                out_slab_send.at[i],
                out_slab_recv.at[spot],
                level * plane + other,
                core,
            )
        )
        out_sends[-1].start()
    out_own = pltpu.make_async_copy(out_weight, out_slab.at[spot], out_slab_local)
    out_own.start()

    first_patch = 4 * lax.broadcasted_iota(jnp.int32, (rows, 4 * rows), 0)
    patch = lax.broadcasted_iota(jnp.int32, (rows, 4 * rows), 1)
    inside = (patch >= first_patch) & (patch < first_patch + 4)
    averaging = jnp.where(inside, 0.25, 0.0).astype(BF16)
    for i in range(width // 512):
        cols = slice(i * 512, (i + 1) * 512)
        blocks[level, :, cols] = dot(averaging, context[:, cols]).astype(BF16)

    def hand(part, send, recv, to_level):
        return remote(part, part, send, recv, to_level * plane + spot, core)

    def near_copies(buffer, send, recv):
        own = buffer.at[level]
        for d in (1, 2):
            yield level + d < depth, hand(own, send.at[d - 1, 0], recv.at[level], level + d)
            yield level - d >= 0, hand(own, send.at[d - 1, 1], recv.at[level], level - d)

    def near_start(buffer, send, recv):
        for there, copy in near_copies(buffer, send, recv):
            pl.when(there)(copy.start)

    def near_sent(buffer, send, recv):
        for there, copy in near_copies(buffer, send, recv):
            pl.when(there)(copy.wait_send)

    def hop_copies(buffer, send, recv, hop):
        up, down = level + 1 < depth, level - 1 >= 0
        if hop == 1:
            own = buffer.at[level]
            yield up, hand(own, send.at[0, 0], recv.at[level], level + 1)
            yield down, hand(own, send.at[0, 1], recv.at[level], level - 1)
        else:
            below, above = buffer.at[level - 1], buffer.at[level + 1]
            yield up & down, hand(below, send.at[1, 0], recv.at[level - 1], level + 1)
            yield up & down, hand(above, send.at[1, 1], recv.at[level + 1], level - 1)

    def hop_start(buffer, send, recv, hop):
        for there, copy in hop_copies(buffer, send, recv, hop):
            pl.when(there)(copy.start)

    def hop_sent(buffer, send, recv):
        for hop in (1, 2):
            for there, copy in hop_copies(buffer, send, recv, hop):
                pl.when(there)(copy.wait_send)

    def far_copies(buffer, send, far_recv):
        pieces = far_recv.shape[0]
        size = buffer.shape[-1] // pieces
        for here, at, to in ((2, 0, 3), (1, 3, 0)):
            for i in range(pieces):
                part = buffer.at[at, ..., pl.ds(i * size, size)]
                yield level == here, hand(part, send.at[i], far_recv.at[i], to)

    def far_start(buffer, recv, send, far_recv):
        @pl.when(level == 2)
        def _():
            arrive(buffer.at[0], recv.at[0])

        @pl.when(level == 1)
        def _():
            arrive(buffer.at[3], recv.at[3])

        for there, copy in far_copies(buffer, send, far_recv):
            pl.when(there)(copy.start)

    def far_sent(buffer, send, far_recv):
        for there, copy in far_copies(buffer, send, far_recv):
            pl.when(there)(copy.wait_send)

    def near_arrive(buffer, recv, d):
        @pl.when((level - d >= 0) & ((d == 1) | (level == 3)))
        def _():
            arrive(buffer.at[level - d], recv.at[level - d])

        @pl.when((level + d < depth) & ((d == 1) | (level == 0)))
        def _():
            arrive(buffer.at[level + d], recv.at[level + d])

    def far_arrive(buffer, far_recv, i):
        size = buffer.shape[-1] // far_recv.shape[0]
        for here, at in ((0, 3), (3, 0)):

            @pl.when(level == here)
            def _():
                arrive(buffer.at[at, ..., pl.ds(i * size, size)], far_recv.at[i])

    near_start(blocks, block_send, block_recv)

    for i in range(width // 512):
        cols = slice(i * 512, (i + 1) * 512)
        mean_residual[:, cols] = dot(averaging, residual[:, cols])

    own_gain = gain[:, pl.ds(pl.multiple_of(core * width, width), width)]

    def squares_of(values):
        return jnp.broadcast_to(
            jnp.sum(values * values, axis=-1, keepdims=True), (values.shape[0], 128)
        )

    def share_squares(buffer, i):
        copy = remote(
            buffer.at[0], buffer.at[1], square_send.at[i], square_recv.at[i], req, sibling
        )
        copy.start()
        copy.wait()
        mean_square = (buffer[0, :, :1] + buffer[1, :, :1]) / (width * cores)
        return lax.rsqrt(mean_square + 1e-05)

    squares[0] = squares_of(prompt[...].astype(F32))
    factor = share_squares(squares, 0)
    for i in range(width // 512):
        cols = slice(i * 512, (i + 1) * 512)
        texts[spot, core, :, cols] = (
            prompt[:, cols].astype(F32) * factor * own_gain[:, cols]
        ).astype(BF16)
    sources[spot] = jnp.broadcast_to(slot_from[...], sources.shape[1:]).astype(BF16)

    far_start(blocks, block_recv, block_far_send, block_far_recv)
    near_arrive(blocks, block_recv, 1)
    near_arrive(blocks, block_recv, 2)
    far_arrive(blocks, block_far_recv, 0)

    slab_own.wait()
    for other in others:
        arrive(slab.at[level, other], slab_in_recv.at[other])
    hop_start(slab, slab_send, slab_recv, 1)

    out_own.wait()
    for other in others:
        arrive(out_slab.at[other], out_slab_recv.at[other])

    def part_of(buffer, place, part, i):
        if i is None:
            return buffer.at[place, part]
        size = buffer.shape[2] // 2
        return buffer.at[place, part, pl.ds(i * size, size)]

    def spread(half_index, buffer, send, recv):
        copies = []
        for i, other in enumerate(others):
            own = part_of(buffer, spot, core, half_index)
            copies.append(
                remote(own, own, send.at[i], recv.at[spot, core], level * plane + other, core)
            )
            copies[-1].start()
        return copies

    def cross(half_index, buffer, place, send, recv):
        part = part_of(buffer, place, core, half_index)
        copy = remote(part, part, send, recv.at[place, core], req, sibling)
        copy.start()
        return copy

    sends = []
    for i, other in enumerate(others):
        own = sources.at[spot]
        sends.append(
            remote(
                own, own, source_send.at[i], source_recv.at[spot], level * plane + other, core
            )
        )
        sends[-1].start()
    sends.extend(spread(0, texts, text_send.at[0], text_recv.at[0]))

    owner_core = level // held
    lane = level % held

    @pl.loop(0, depth)
    def _(step):
        target = (level + 1 + step) % depth
        for i in range(plane):
            partials[target, :, i * columns : (i + 1) * columns] = dot(
                blocks[target], out_slab[i]
            ).astype(BF16)
        own = (target == level) & (owner_core == core)

        @pl.when(own)
        def _():
            pltpu.make_async_copy(
                partials.at[target], returned.at[lane, core], partial_recv.at[lane, core]
            ).start()

        @pl.when(jnp.logical_not(own))
        def _():
            remote(
                partials.at[target],
                returned.at[lane, core],
                partial_send.at[target],
                partial_recv.at[lane, core],
                target * plane + spot,
                owner_core,
            ).start()

    for i in range(held):
        for j in range(cores):
            arrive(returned.at[i, j], partial_recv.at[i, j])
    for i in range(held):
        cols = slice(i * half, (i + 1) * half)
        added = returned[i, 0].astype(F32)
        for j in range(1, cores):
            added = added + returned[i, j].astype(F32)
        merged[:, cols] = (mean_residual[:, cols] + scale[:, cols] * added).astype(BF16)

    block_rows = outgoing.shape[1]
    slot = lax.broadcasted_iota(jnp.int32, (requests * block_rows, rows), 0)
    placed = jnp.zeros((requests * block_rows, half), F32)
    for i in range(2):
        place = jnp.where(slot == target_row[...] + i * (block_rows // 2), 1.0, 0.0).astype(BF16)
        placed = placed + dot(place, merged[:, i * half : (i + 1) * half])
    outgoing[...] = placed.astype(BF16).reshape(outgoing.shape)

    @pl.loop(1, requests)
    def _(offset):
        to = (req + offset) % requests
        remote(
            outgoing.at[to], arrived.at[req], place_send.at[to], place_recv.at[req], to, core
        ).start()

    place_own = pltpu.make_async_copy(outgoing.at[req], arrived.at[req], place_send.at[req])
    place_own.start()
    sends.extend(spread(1, texts, text_send.at[1], text_recv.at[1]))
    near_arrive(slab, slab_recv, 1)
    hop_start(slab, slab_send, slab_recv, 2)
    place_own.wait()

    @pl.loop(1, requests)
    def _(offset):
        source = (req + offset) % requests
        arrive(arrived.at[source], place_recv.at[source])

    slot = lax.broadcasted_iota(jnp.int32, (images.shape[0], requests * block_rows), 1)
    for i in range(2):
        pick = jnp.where(slot == image_from[...] + i * (block_rows // 2), 1.0, 0.0).astype(BF16)
        images[:, i * half : (i + 1) * half] = dot(
            pick, arrived[...].reshape(requests * block_rows, half)
        )
    image_squares[0] = squares_of(images[...])
    factor = share_squares(image_squares, 1)
    for i in range(2):
        cols = slice(i * half, (i + 1) * half)
        pictures[spot, core, :, cols] = (images[:, cols] * factor * own_gain[:, cols]).astype(BF16)
    sends.extend(spread(None, pictures, picture_send, picture_recv))
    sends.append(cross(None, pictures, spot, picture_cross.at[0], picture_recv))
    for h in range(2):
        sends.append(cross(h, texts, spot, text_cross.at[h, 0], text_recv.at[h]))
    far_start(slab, slab_recv, slab_far_send, slab_far_recv)

    def hand_over(h, buffer, send, recv):
        for i, other in enumerate(others):
            arrive(part_of(buffer, other, core, h), recv.at[other, core])
            sends.append(cross(h, buffer, other, send.at[i + 1], recv))

    for other in others:
        arrive(sources.at[other], source_recv.at[other])
    hand_over(0, texts, text_cross.at[0], text_recv.at[0])
    hand_over(1, texts, text_cross.at[1], text_recv.at[1])
    hand_over(None, pictures, picture_cross, picture_recv)
    for place in [spot] + others:
        for h in range(2):
            arrive(part_of(texts, place, sibling, h), text_recv.at[h, place, sibling])
        arrive(pictures.at[place, sibling], picture_recv.at[place, sibling])

    tile = 256
    level_rows = plane * depth_rows
    seq_texts = texts.shape[2]
    lanes = lax.broadcasted_iota(jnp.int32, (seq, 128), 1).astype(F32)

    def level_of(at, place):
        part = at // held
        base = pl.multiple_of((at % held) * level_rows, level_rows)
        source = sources[place].astype(F32)
        picks = [
            jnp.where(source == lanes + i * 128, 1.0, 0.0).astype(BF16)
            for i in range(seq_texts // 128)
        ]
        image_pick = jnp.where(source == -1.0 - lanes, 1.0, 0.0).astype(BF16)
        text_pick = jnp.concatenate(picks, axis=1)
        a = dot(text_pick, texts[place, part, :, pl.ds(base, level_rows)]) + dot(
            image_pick, pictures[place, part, :, pl.ds(base, level_rows)]
        )
        return a.astype(BF16)

    def multiply_all(at, first):
        @pl.loop(0, plane)
        def _(place):
            a = level_of(at, place)
            for n in range(share // tile):
                cols = slice(n * tile, (n + 1) * tile)
                b = slab[at, :, :, cols].reshape(level_rows, tile)
                if first:
                    total[place, :, cols] = dot(a, b)
                else:
                    total[place, :, cols] += dot(a, b)

    multiply_all(level, True)
    for d in (1, 2):
        if d == 2:
            near_arrive(slab, slab_recv, d)

        @pl.when(level - d >= 0)
        def _():
            multiply_all(level - d, False)

        @pl.when(level + d < depth)
        def _():
            multiply_all(level + d, False)

    at_edge = (level == 0) | (level == depth - 1)
    last = depth - 1 - level

    @pl.when(at_edge)
    def _():
        @pl.loop(0, plane)
        def _(place):
            assembled[place] = level_of(last, place)

    def leave(place, n):
        start = pl.multiple_of(spot * share + n * tile, tile)
        return remote(
            turned.at[place, :, pl.ds(n * tile, tile)],
            out.at[:, pl.ds(start, tile)],
            turned_send.at[place, n],
            turned_recv.at[spot, n],
            level * plane + place,
            core,
        )

    for n in range(share // tile):
        far_arrive(slab, slab_far_recv, n)

        @pl.loop(0, plane)
        def _(step):
            place = (spot + 1 + step) % plane

            @pl.when(at_edge)
            def _():
                cols = slice(n * tile, (n + 1) * tile)
                b = slab[last, :, :, cols].reshape(level_rows, tile)
                total[place, :, cols] += dot(assembled[place], b)

            for head in range(n * tile // HEAD, (n + 1) * tile // HEAD):
                cols = slice(head * HEAD, (head + 1) * HEAD)
                values = total[place, :, cols]
                if head <= GROUP:
                    values = values * cosine[...] + pltpu.roll(values, HEAD // 2, 1) * sine[...]
                turned[place, :, cols] = values.astype(BF16)

            @pl.when(step < plane - 1)
            def _():
                leave(place, n).start()

    here = pl.ds(pl.multiple_of(spot * share, share), share)
    turned_own = pltpu.make_async_copy(turned.at[spot], out.at[:, here], turned_local)
    turned_own.start()

    for copy in out_sends + slab_sends + sends:
        copy.wait_send()
    near_sent(blocks, block_send, block_recv)
    far_sent(blocks, block_far_send, block_far_recv)
    hop_sent(slab, slab_send, slab_recv)
    far_sent(slab, slab_far_send, slab_far_recv)

    @pl.loop(0, depth)
    def _(target):
        @pl.when(jnp.logical_not((target == level) & (owner_core == core)))
        def _():
            remote(
                partials.at[target],
                returned.at[lane, core],
                partial_send.at[target],
                partial_recv.at[lane, core],
                req,
                sibling,
            ).wait_send()

    @pl.loop(1, requests)
    def _(offset):
        to = (req + offset) % requests
        remote(
            outgoing.at[to], arrived.at[req], place_send.at[to], place_recv.at[req], req, sibling
        ).wait_send()

    for other in others:
        for n in range(share // tile):
            leave(other, n).wait_send()
    turned_own.wait()
    for other in others:
        for n in range(share // tile):
            start = pl.multiple_of(other * share + n * tile, tile)
            arrive(out.at[:, pl.ds(start, tile)], turned_recv.at[other, n])


def fused_shards(
    vit_context,
    vision_residual,
    out_weight,
    layer_scale,
    prompt,
    prompt_len,
    image_at,
    grid_sizes,
    image_owner,
    norm_gain,
    qkv_weight,
):
    requests = lax.axis_size("req")
    cores = lax.axis_size("tp")
    device_index = lax.axis_index("req")
    tp_index = lax.axis_index("tp")
    patches, width = vit_context.shape
    rows = patches // 4
    share = (GROUP + 2) * HEAD
    plane = qkv_weight.shape[1] // share
    depth = requests // plane
    seq_slots = prompt.shape[1] + IMG_MAX

    counts, starts = request_plan(grid_sizes, image_owner, requests)
    request_ends = starts + counts
    capacity = (IMG_MAX + requests - 1) // requests
    request_ids = jnp.arange(requests, dtype=jnp.int32)
    group_index = jnp.arange(rows, dtype=jnp.int32) * requests + device_index
    destination = jnp.sum((request_ends[None, :] <= group_index[:, None]).astype(jnp.int32), axis=1)
    owned_start = jnp.sum(
        jnp.where(destination[:, None] == request_ids[None, :], starts[None, :], 0), axis=1
    )
    target = destination * 2 * capacity + (group_index - owned_start) // requests
    usable = destination < requests
    target = jnp.where(usable, target, -requests * 2 * capacity)
    own_request = request_ids == device_index
    own_count = jnp.sum(jnp.where(own_request, counts, 0))
    own_start = jnp.sum(jnp.where(own_request, starts, 0))
    image_from = image_at[0]
    prompt_count = prompt_len[0]
    image_row = jnp.arange(IMG_MAX, dtype=jnp.int32)
    from_flat = (own_start + image_row) % requests * 2 * capacity + image_row // requests
    from_flat = jnp.where(image_row < own_count, from_flat, -requests * 2 * capacity)
    slot_index = jnp.arange(seq_slots, dtype=jnp.int32)
    slot_image = slot_index - image_from
    in_image = (slot_image >= 0) & (slot_image < own_count)
    slot_row = jnp.where(slot_index < image_from, slot_index, slot_index - own_count)
    slot_from = jnp.where(slot_index < prompt_count + own_count, slot_row, 512)
    slot_from = jnp.where(in_image, -1 - slot_image, slot_from)
    cosine_table, sine_table = rope_tables(seq_slots)
    cosine = jnp.concatenate([cosine_table, cosine_table], axis=1)
    sine = jnp.concatenate([-sine_table, sine_table], axis=1)

    vmem = pl.BlockSpec(memory_space=pltpu.VMEM)
    anywhere = pl.BlockSpec(memory_space=pl.ANY)
    dma = pltpu.SemaphoreType.DMA
    columns = out_weight.shape[1]
    half = width // 2
    return pl.pallas_call(
        functools.partial(fused_kernel, (requests, cores, plane, depth)),
        out_shape=jax.ShapeDtypeStruct((seq_slots, qkv_weight.shape[1]), BF16),
        in_specs=[vmem, vmem, anywhere, vmem, vmem, vmem, anywhere] + [vmem] * 5,
        out_specs=anywhere,
        scratch_shapes=[
            pltpu.VMEM((depth, plane, qkv_weight.shape[0], share), BF16),
            pltpu.VMEM((plane, width, columns), BF16),
            pltpu.VMEM((depth, rows, width), BF16),
            pltpu.VMEM((depth, rows, plane * columns), BF16),
            pltpu.VMEM((depth // cores, cores, rows, plane * columns), BF16),
            pltpu.VMEM((rows, width), F32),
            pltpu.VMEM((rows, width), BF16),
            pltpu.VMEM((requests, 2 * capacity, half), BF16),
            pltpu.VMEM((requests, 2 * capacity, half), BF16),
            pltpu.VMEM((IMG_MAX, width), F32),
            pltpu.VMEM((2, prompt.shape[1], 128), F32),
            pltpu.VMEM((2, IMG_MAX, 128), F32),
            pltpu.VMEM((plane, cores, prompt.shape[1], width), BF16),
            pltpu.VMEM((plane, cores, IMG_MAX, width), BF16),
            pltpu.VMEM((plane, seq_slots, 128), BF16),
            pltpu.VMEM((plane, seq_slots, share), F32),
            pltpu.VMEM((plane, seq_slots, share), BF16),
            pltpu.VMEM((plane, seq_slots, plane * qkv_weight.shape[0]), BF16),
            dma((plane,)),
            dma((plane,)),
            dma,
            dma((depth, 2)),
            dma((depth,)),
            dma((plane,)),
            dma((plane,)),
            dma,
            dma((depth, 2)),
            dma((depth,)),
            dma((depth,)),
            dma((depth // cores, cores)),
            dma((requests,)),
            dma((requests,)),
            dma((2,)),
            dma((2,)),
            dma((2, plane)),
            dma((2, plane, cores)),
            dma((2, plane)),
            dma((plane,)),
            dma((plane, cores)),
            dma((plane,)),
            dma((plane,)),
            dma((plane,)),
            dma((plane, 3)),
            dma((plane, 3)),
            dma,
            dma((3,)),
            dma((3,)),
            dma((1,)),
            dma((1,)),
        ],
        compiler_params=pltpu.CompilerParams(
            collective_id=0, has_side_effects=True, vmem_limit_bytes=58 * 1024 * 1024
        ),
        cost_estimate=pl.CostEstimate(
            flops=30 * 10**9, bytes_accessed=20 * 2**20, transcendentals=0
        ),
    )(
        vit_context,
        vision_residual,
        out_weight,
        layer_scale[None, :],
        prompt[0],
        norm_gain[None, :],
        qkv_weight,
        target[None, :],
        from_flat[:, None],
        slot_from[:, None],
        cosine,
        sine,
    )


def solution(mesh):
    requests, cores = mesh.shape["req"], mesh.shape["tp"]

    def shards(*arrays):
        patches, width = arrays[0].shape
        plane = arrays[-1].shape[1] // ((GROUP + 2) * HEAD)
        fits = (
            cores == 2
            and plane == 4
            and requests // plane == 4
            and arrays[2].shape[1] * requests == width * cores
            and arrays[2].shape[1] % 128 == 0
            and IMG_MAX % requests == 0
            and (IMG_MAX // requests) % 8 == 0
            and IMG_MAX == 128
            and arrays[4].shape[1] in (128, 256)
        )
        return (fused_shards if fits else collective_shards)(*arrays)

    in_specs = (
        P("req", "tp"),
        P("req", "tp"),
        P("tp", "req"),
        P("tp"),
        P("req", None, "tp"),
        P("req"),
        P("req"),
        P(),
        P(),
        P(),
        P("req", "tp"),
    )
    out_specs = P("req", "tp")
    return jax.shard_map(shards, mesh=mesh, in_specs=in_specs, out_specs=out_specs, check_vma=False)
```
